128 devices in a mesh: dp: 2 (over x_hi), ctx: 8 (over z, x_lo), tensor: 8 (over y, core).
Axes of the slice: x: 4 (x_hi: 2, x_lo: 2; x = x_hi * 2 + x_lo), y: 4, z: 4, core: 2. Of those that a mesh axis runs over, the one named last changes fastest.
Arguments:
- tokens: bfloat16 [2048, 3072], P(('dp', 'ctx'), 'tensor'), may hold values from -6 to 6
- d_out: bfloat16 [2048, 3072], P(('dp', 'ctx'), 'tensor'), may hold values from -6 to 6
- routes: int32 [2048, 2], P(('dp', 'ctx')), may hold values from 0 to 7, all different within a row; in each aligned block of 128 rows (0 to 127, 128 to 255, ...) at most 64 rows name the same one
- probs: bfloat16 [2048, 2], P(('dp', 'ctx')), may hold values from 0.049804688 to 1
- w_gate: bfloat16 [8, 3072, 8192], P('ctx', None, ('dp', 'tensor')), may hold values from -0.109375 to 0.109375
- w_up: bfloat16 [8, 3072, 8192], P('ctx', None, ('dp', 'tensor')), may hold values from -0.109375 to 0.109375
- w_down: bfloat16 [8, 8192, 3072], P('ctx', ('dp', 'tensor')), may hold values from -0.0625 to 0.0625
Outputs:
- d_tokens: bfloat16 [2048, 3072], P(('dp', 'ctx'), 'tensor')
- d_probs: float32 [2048, 2], P(('dp', 'ctx'))
- grad_gate: bfloat16 [8, 3072, 8192], P('ctx', None, ('dp', 'tensor'))
- grad_up: bfloat16 [8, 3072, 8192], P('ctx', None, ('dp', 'tensor'))
- grad_down: bfloat16 [8, 8192, 3072], P('ctx', ('dp', 'tensor'))
The draws below stay inside these ranges and needn't reach their ends.
Inputs may be any that keep to these rules, and one draw needn't show every extreme that they name: `routes`: the two experts of a token differ. Among the 128 tokens of one device no expert is named more than 64 times, a bound that some block reaches.
All inputs are finite; a program needn't handle non-finite values.
Results may differ from the reference program's by a relative error of at most 0.0075.
Values may be sent and summed in bfloat16 or wider, within the bound.
No kernel may reach another device: no remote copies, remote signals or barrier semaphores. Data moves between devices by JAX's collectives and lax.ppermute only.
A program may use at most 128 MiB of HBM per device.

```python
import math
import jax
import jax.numpy as jnp
import numpy as np
from jax import lax

D = 3072
FF = 8192
TOK_DEV = 128
TOP = 2
EXPERTS = 8
CAP = 64
ROWS = 1024
TOKENS = 2048


def level_of(stream_key, extent, pieces, smallest, high):
    def one(axis_at, parts):
        heights = jax.random.uniform(jax.random.fold_in(jax.random.fold_in(stream_key, 6), axis_at), (parts,), jnp.float32, smallest / len(pieces), high / len(pieces))
        return jnp.repeat(jnp.exp(heights), extent[axis_at] // parts).reshape((-1,) + (1,) * (len(extent) - axis_at - 1))

    factor_of = one(*pieces[0])
    for cut in pieces[1:]:
        factor_of = factor_of * one(*cut)
    return factor_of


def routed_block(rng, own, number, rows, amount, top, bound, lean):
    order = jax.random.permutation(rng, amount)
    heavy_load, ordinary = load_shares(amount, rows * top, bound, lean, True), load_shares(amount, rows * top, bound, lean, False)
    places = jnp.arange(amount)

    def named(sizes, rotation):
        used = int((sizes > 0).sum())
        fixed = max(1, used // 4)
        moved = fixed + (places - fixed + rotation * (used - fixed)) % max(1, amount - fixed)
        return jnp.zeros((amount,), jnp.int32).at[order[jnp.where(places < fixed, places, moved)]].set(jnp.asarray(sizes, jnp.int32))

    sizes = jnp.where(number % 4 == 0, named(heavy_load, number // 4), named(ordinary, number - number // 4 - 1))
    mixed = jax.random.permutation(jax.random.fold_in(own, 3), amount)
    donor, receiver = mixed[0:amount // 2 * 2:2], mixed[1:amount // 2 * 2:2]
    room = jnp.minimum(sizes[donor] - 1, bound - sizes[receiver]) // 2
    room = jnp.where((donor == order[0]) | (receiver == order[0]) | (sizes[receiver] == 0), 0, jnp.maximum(room, 0))
    moved = jax.random.randint(jax.random.fold_in(own, 4), (amount // 2,), 0, 1 << 20) % (room + 1)
    sizes = sizes.at[donor].add(-moved).at[receiver].add(moved)
    items = jnp.searchsorted(jnp.cumsum(sizes), jnp.arange(rows * top), side="right").astype(jnp.int32)
    listing = items.reshape(top, rows).T
    listing = listing[jax.random.permutation(jax.random.fold_in(own, 1), rows)]
    rotation = jax.random.randint(jax.random.fold_in(own, 2), (rows, 1), 0, top)
    return jnp.take_along_axis(listing, (jnp.arange(top)[None, :] + rotation) % top, axis=1)


def load_shares(number_of, total, most, lean, full):
    weights = [(1 << 20) // math.isqrt(grade ** lean) + 1 for grade in range(1, number_of + 1)]
    largest = most if full else min(most, max(-(-total // number_of), total * weights[0] // sum(weights)))
    least = 1 if total - largest >= number_of - 1 else 0
    holding, rest = [largest] + [least] * (number_of - 1), total - largest - least * (number_of - 1)
    while rest > 0:
        free = [i for i in range(1, number_of) if holding[i] < largest] or [i for i in range(1, number_of) if holding[i] < most]
        whole, budget = sum([weights[i] for i in free]), rest
        for i in free:
            extra = min(most - holding[i], max(1, budget * weights[i] // whole), rest)
            holding[i] = holding[i] + extra
            rest = rest - extra
    return np.array(holding)


def gaussian(own_key, shape, deviation, reach, split=(), held_as=jnp.bfloat16):
    drawn = jax.random.normal(own_key, shape, jnp.float32) * deviation
    if len(split) > 0:
        drawn = level_of(own_key, shape, split, -0.22, 0.18) * drawn
    return jnp.clip(drawn, min=-reach, max=reach).astype(held_as)


def setup_inputs(seed: int = 0) -> dict:
    arg_keys = jax.random.split(jax.random.key(seed), 8)
    tokens = gaussian(arg_keys[0], (TOKENS, D), 1.0, 6.0, ((0, 16), (1, 8)))
    d_out = gaussian(arg_keys[1], (TOKENS, D), 1.0, 6.0, ((0, 16), (1, 8)))
    routes_keys = jax.random.split(jax.random.fold_in(arg_keys[2], 1), TOKENS // TOK_DEV)
    routes_turns = jax.random.permutation(jax.random.fold_in(arg_keys[2], 3), TOKENS // TOK_DEV)
    routes = jax.vmap(lambda own, number: routed_block(jax.random.fold_in(arg_keys[2], 2), own, number, TOK_DEV, EXPERTS, TOP, CAP, 2))(routes_keys, routes_turns).reshape((TOKENS, TOP))
    probs = jnp.clip(jnp.exp(math.log(1.0) - 2.9996462 * jax.random.uniform(arg_keys[3], (TOKENS, TOP), jnp.float32) ** level_of(arg_keys[3], (TOKENS, TOP), ((0, 16),), -0.2, 0.2)), 0.049804688, 1.0).astype(jnp.bfloat16)
    w_gate = gaussian(arg_keys[4], (EXPERTS, D, FF), D ** -0.5, 0.109375, ((0, 8), (2, 16)))
    w_up = gaussian(arg_keys[5], (EXPERTS, D, FF), D ** -0.5, 0.109375, ((0, 8), (2, 16)))
    w_down = gaussian(arg_keys[6], (EXPERTS, FF, D), FF ** -0.5, 0.0625, ((0, 8), (1, 16)))
    return {"tokens": tokens, "d_out": d_out, "routes": routes, "probs": probs, "w_gate": w_gate, "w_up": w_up, "w_down": w_down}


def silu_parts(pre_gate):
    sigma = jax.nn.sigmoid(pre_gate)
    return pre_gate * sigma, sigma * (1.0 + pre_gate * (1.0 - sigma))


def expert_rows(rows_in, grads_in, weights_row, gate_weight, up_weight, down_weight):
    pre_gate = jnp.dot(rows_in, gate_weight, preferred_element_type=jnp.float32)
    pre_up = jnp.dot(rows_in, up_weight, preferred_element_type=jnp.float32)
    active, slope = silu_parts(pre_gate)
    hidden = (active * pre_up).astype(jnp.bfloat16)
    backward = lax.dot_general(grads_in, down_weight, (((1,), (1,)), ((), ())), preferred_element_type=jnp.float32)
    prob_grad = jnp.sum(hidden.astype(jnp.float32) * backward, axis=1)
    hidden_grad = weights_row[:, None] * backward
    gate_grad = (hidden_grad * pre_up * slope).astype(jnp.bfloat16)
    up_grad = (hidden_grad * active).astype(jnp.bfloat16)
    scaled = (weights_row[:, None] * hidden.astype(jnp.float32)).astype(jnp.bfloat16)
    return gate_grad, up_grad, prob_grad, scaled


def weight_grads(rows_in, grads_in, gate_grad, up_grad, scaled):
    contract = (((0,), (0,)), ((), ()))
    gate_total = lax.dot_general(rows_in, gate_grad, contract, preferred_element_type=jnp.float32)
    up_total = lax.dot_general(rows_in, up_grad, contract, preferred_element_type=jnp.float32)
    down_total = lax.dot_general(scaled, grads_in, contract, preferred_element_type=jnp.float32)
    return gate_total, up_total, down_total


def reference(tokens, d_out, routes, probs, w_gate, w_up, w_down):
    flat_ids = routes.reshape(-1)
    flat_probs = probs.reshape(-1).astype(jnp.float32)
    transpose_contract = (((1,), (1,)), ((), ()))

    def per_expert(carry, expert):
        assign_grad, prob_grads = carry
        others = (flat_ids != expert).astype(jnp.int32)
        order = jnp.argsort(others, stable=True)[:ROWS].astype(jnp.int32)
        count = jnp.sum(1 - others)
        valid = jnp.arange(ROWS, dtype=jnp.int32) < count
        token_of = order // 2
        rows_in = tokens[token_of]
        grads_in = d_out[token_of]
        weights_row = jnp.where(valid, flat_probs[order], jnp.zeros_like(flat_probs[order]))
        gate_weight = w_gate[expert]
        up_weight = w_up[expert]
        down_weight = w_down[expert]
        gate_grad, up_grad, prob_grad, scaled = expert_rows(rows_in, grads_in, weights_row, gate_weight, up_weight, down_weight)
        partial_rows = lax.dot_general(gate_grad, gate_weight, transpose_contract, preferred_element_type=jnp.float32)
        partial_rows = partial_rows + lax.dot_general(up_grad, up_weight, transpose_contract, preferred_element_type=jnp.float32)
        assign_grad = assign_grad.at[order].add(partial_rows)
        prob_grads = prob_grads.at[order].add(jnp.where(valid, prob_grad, jnp.zeros_like(prob_grad)))
        gate_total, up_total, down_total = weight_grads(rows_in, grads_in, gate_grad, up_grad, scaled)
        return (assign_grad, prob_grads), (gate_total.astype(jnp.bfloat16), up_total.astype(jnp.bfloat16), down_total.astype(jnp.bfloat16))

    initial = (jnp.zeros((2 * TOKENS, D), jnp.float32), jnp.zeros((2 * TOKENS,), jnp.float32))
    (assign_grad, prob_grads), (grad_gate, grad_up, grad_down) = lax.scan(per_expert, initial, jnp.arange(EXPERTS, dtype=jnp.int32))
    d_tokens = jnp.sum(assign_grad.reshape(TOKENS, 2, D), axis=1).astype(jnp.bfloat16)
    d_probs = prob_grads.reshape(TOKENS, 2)
    return d_tokens, d_probs, grad_gate, grad_up, grad_down
```

```python
import jax
import jax.numpy as jnp
from jax import lax
from jax.experimental import pallas as pl
from jax.experimental.pallas import tpu as pltpu
from jax.sharding import PartitionSpec as P

BF = jnp.bfloat16
F32 = jnp.float32
VMEM_LIMIT = 56 * 1024 * 1024
EXPERTS = 8
CAP = 64
TOK = 128
COLS = 384
ROWS = 1024
HID = 512
NT = (((1,), (1,)), ((), ()))
TN = (((0,), (0,)), ((), ()))


def dot(a, b, dims=(((1,), (0,)), ((), ()))):
    return lax.dot_general(a, b, dims, preferred_element_type=F32)


def call(body, outs, grid=None, scratch=(), flops=0, nbytes=0, **specs):
    params = dict(vmem_limit_bytes=VMEM_LIMIT)
    return pl.pallas_call(
        body,
        out_shape=outs,
        compiler_params=pltpu.CompilerParams(**params),
        cost_estimate=pl.CostEstimate(flops=flops, bytes_accessed=nbytes, transcendentals=0),
        **specs,
    )


def sds(shape, dtype=BF):
    return jax.ShapeDtypeStruct(shape, dtype)


def slot_masks(routes):
    expert = lax.broadcasted_iota(jnp.int32, (EXPERTS, TOK), 0)
    first = routes[0:1, :] == expert
    second = routes[1:2, :] == expert
    named = jnp.where(first | second, 1.0, 0.0).astype(F32)
    before = lax.broadcasted_iota(jnp.int32, (TOK, TOK), 0)
    after = lax.broadcasted_iota(jnp.int32, (TOK, TOK), 1)
    earlier = jnp.where(before < after, 1.0, 0.0).astype(BF)
    rank = dot(named.astype(BF), earlier)
    slot = jnp.where(named > 0.0, rank, -1.0)
    return first, second, slot


def one_hot(slot, expert):
    place = lax.broadcasted_iota(jnp.int32, (CAP, TOK), 0).astype(F32)
    return jnp.where(slot[expert : expert + 1, :] == place, 1.0, 0.0)


def dispatch_x_body(routes, tokens, out):
    _, _, slot = slot_masks(routes[...])
    select = jnp.concatenate([one_hot(slot, e) for e in range(EXPERTS)], axis=0).astype(BF)
    rows = dot(select, tokens[...]).astype(BF).reshape(EXPERTS, CAP, COLS)
    out[0:EXPERTS] = rows
    out[EXPERTS : 2 * EXPERTS] = rows


def dispatch_g_body(routes, probs, g0, g1, g2, g3, out):
    first, _, slot = slot_masks(routes[...])
    weight = jnp.where(first, probs[0:1, :], probs[1:2, :])
    select = jnp.concatenate(
        [one_hot(slot, e) * weight[e : e + 1, :] for e in range(EXPERTS)], axis=0
    ).astype(BF)
    for i, g in enumerate((g0, g1, g2, g3)):
        rows = dot(select, g[...]).astype(BF).reshape(EXPERTS, CAP, COLS)
        out[0:EXPERTS, :, i * COLS : (i + 1) * COLS] = rows
        out[EXPERTS : 2 * EXPERTS, :, i * COLS : (i + 1) * COLS] = rows


def slice_of(t, dy, sibling):
    core = t % 2
    core = 1 - core if sibling else core
    return ((t // 2 + dy) % 4) * 2 + core


def plain_call(body, t, ins, outs, scratch, copies, flops, nbytes):
    anywhere = pl.BlockSpec(memory_space=pltpu.HBM)
    return pl.pallas_call(
        body,
        out_shape=outs,
        in_specs=[pl.BlockSpec(memory_space=pltpu.SMEM)] + [anywhere] * len(ins),
        out_specs=[anywhere] * len(outs),
        scratch_shapes=[pltpu.VMEM(shape, dtype) for shape, dtype in scratch]
        + [pltpu.SemaphoreType.DMA((copies,))],
        compiler_params=pltpu.CompilerParams(vmem_limit_bytes=VMEM_LIMIT),
        cost_estimate=pl.CostEstimate(flops=flops, bytes_accessed=nbytes, transcendentals=0),
    )(t, *ins)


class Copies:
    def __init__(self, sems):
        self.sems, self.used = sems, 0

    def start(self, src, dst):
        copy = pltpu.make_async_copy(src, dst, self.sems.at[self.used])
        self.used += 1
        copy.start()
        return copy


def wait_all(copies):
    for copy in copies:
        copy.wait()


def slice_at(t, dy, sibling):
    return pl.ds(pl.multiple_of(slice_of(t[0], dy, sibling) * COLS, COLS), COLS)


def lanes(dy):
    return slice(dy * COLS, (dy + 1) * COLS)


def down_columns(copies, t, wd, into, sibling):
    return [
        copies.start(
            wd.at[:, pl.ds(pl.multiple_of(slice_of(t[0], dy, sibling) * COLS, 128), COLS)],
            into.at[:, lanes(dy)],
        )
        for dy in range(4)
    ]


def gate_up_rows(copies, t, wg, wu, into, steps, sibling):
    started = []
    for i, dy in enumerate(steps):
        at = slice_at(t, dy, sibling)
        started.append(copies.start(wg.at[at, :], into.at[lanes(i), 0:HID]))
        started.append(copies.start(wu.at[at, :], into.at[lanes(i), HID : 2 * HID]))
    return started


def chunks(rows):
    return [slice(r, r + rows) for r in range(0, ROWS, rows)]


def back_own_body(t, g, wd, out, g_v, w_v, out_v, sems):
    copies = Copies(sems)
    w_in = down_columns(copies, t, wd, w_v, False)
    g_in = [copies.start(g.at[c], g_v.at[c]) for c in chunks(256)]
    wait_all(w_in)
    done = []
    for c, g_copy in zip(chunks(256), g_in):
        g_copy.wait()
        out_v[c] = dot(g_v[c], w_v[...], NT)
        done.append(copies.start(out_v.at[c], out.at[c]))
    wait_all(done)


def split_lanes(value):
    upper = value.astype(BF).astype(F32)
    lower = value - upper
    lane = lax.broadcasted_iota(jnp.int32, (value.shape[0], 128), 1)
    return jnp.where(lane == 0, upper, jnp.where(lane == 1, lower, 0.0)).astype(BF)


def back_body(t, g, own, act, slope, hidden, wd, wg, wu, grads, prob, *refs):
    parts = refs[:4]
    g_v, own_v, act_v, slope_v, hidden_v, wd_v, w_v, grads_v, prob_v, part_v, sems = refs[4:]
    copies = Copies(sems)
    wd_in = down_columns(copies, t, wd, wd_v, True)
    pairs = ((g, g_v), (own, own_v), (act, act_v), (slope, slope_v), (hidden, hidden_v))
    rows = chunks(256)
    ins = [[copies.start(a.at[rows[0]], b.at[rows[0]]) for a, b in pairs]]
    w_in = gate_up_rows(copies, t, wg, wu, w_v, range(4), True)
    ins += [[copies.start(a.at[c], b.at[c]) for a, b in pairs] for c in rows[1:]]
    done = []
    for i, c in enumerate(rows):
        if i == 0:
            wait_all(wd_in)
        wait_all(ins[i])
        back = own_v[c] + dot(g_v[c], wd_v[...], NT)
        prob_v[c] = split_lanes(
            jnp.sum(hidden_v[c].astype(F32) * back, axis=1, keepdims=True)
        )
        grads_v[c, 0:HID] = (back * slope_v[c]).astype(BF)
        grads_v[c, HID : 2 * HID] = (back * act_v[c]).astype(BF)
        if i == 0:
            wait_all(w_in)
        part_v[c] = dot(grads_v[c], w_v[...], NT).astype(BF)
        done.append(copies.start(grads_v.at[c], grads.at[c]))
        done.append(copies.start(prob_v.at[c], prob.at[c]))
        for dy in range(4):
            done.append(copies.start(part_v.at[c, lanes(dy)], parts[dy].at[c]))
    wait_all(done)


def sums_body(t, grads, prob, prob_sib, s1, s2, s3, wg, wu, out1, out2, out3, *refs):
    grads_v, prob_v, sib_v, p1, p2, p3, w_v, o1, o2, o3, sems = refs
    copies = Copies(sems)
    w_in = gate_up_rows(copies, t, wg, wu, w_v, (2, 1, 3), False)
    pairs = ((grads, grads_v), (prob, prob_v), (prob_sib, sib_v), (s2, p2), (s1, p1), (s3, p3))
    rows = chunks(256)
    ins = [[copies.start(a.at[c], b.at[c]) for a, b in pairs] for c in rows]
    wait_all(w_in)
    done = []
    for c, started in zip(rows, ins):
        wait_all(started)
        part = dot(grads_v[c], w_v[...], NT)
        for i, (p, o) in enumerate(((p2, o2), (p1, o1), (p3, o3))):
            o[c, 0:COLS] = (part[:, lanes(i)] + p[c].astype(F32)).astype(BF)
        both = prob_v[c].astype(F32) + sib_v[c].astype(F32)
        o2[c, COLS : COLS + 128] = split_lanes(jnp.sum(both, axis=1, keepdims=True))
        for o, out in ((o2, out2), (o1, out1), (o3, out3)):
            done.append(copies.start(o.at[c], out.at[c]))
    wait_all(done)


def last_sum_body(t, grads, s0, left, right, wg, wu, out, *refs):
    grads_v, s_v, l_v, r_v, w_v, o_v, sems = refs
    copies = Copies(sems)
    w_in = gate_up_rows(copies, t, wg, wu, w_v, (0,), False)
    pairs = ((grads, grads_v), (s0, s_v), (left, l_v), (right, r_v))
    rows = chunks(256)
    ins = [[copies.start(a.at[c], b.at[c]) for a, b in pairs] for c in rows]
    wait_all(w_in)
    done = []
    for c, started in zip(rows, ins):
        wait_all(started)
        part = dot(grads_v[c], w_v[...], NT)
        part += s_v[c].astype(F32) + l_v[c].astype(F32) + r_v[c].astype(F32)
        o_v[c] = part.astype(BF)
        done.append(copies.start(o_v.at[c], out.at[c]))
    wait_all(done)


def forward_body(t, *refs):
    xs, (wg, wu), (act, slope, hidden) = refs[:8], refs[8:10], refs[10:13]
    x_v, wg_v, wu_v, act_v, slope_v, hidden_v, sems = refs[13:]
    copies = Copies(sems)
    rows = chunks(256)

    def x_chunk(c):
        return [
            copies.start(
                x.at[c],
                x_v.at[
                    c,
                    pl.ds(
                        pl.multiple_of(slice_of(t[0], i % 4, i >= 4) * COLS, 128), COLS
                    ),
                ],
            )
            for i, x in enumerate(xs)
        ]

    ins = [x_chunk(rows[0])]
    wg_in = copies.start(wg, wg_v)
    wu_in = copies.start(wu, wu_v)
    ins += [x_chunk(c) for c in rows[1:]]
    done = []
    for i, c in enumerate(rows):
        wait_all(ins[i])
        if i == 0:
            wg_in.wait()
        gate = dot(x_v[c], wg_v[...])
        if i == 0:
            wu_in.wait()
        up = dot(x_v[c], wu_v[...])
        sigma = jax.nn.sigmoid(gate)
        active = gate * sigma
        act_v[c] = active
        slope_v[c] = up * (sigma * (1.0 + gate * (1.0 - sigma)))
        hidden_v[c] = (active * up).astype(BF)
        for a, b in ((act_v, act), (slope_v, slope), (hidden_v, hidden)):
            done.append(copies.start(a.at[c], b.at[c]))
    wait_all(done)


def weights_gate_up_body(t, grads, *refs):
    xs = refs[:8]
    out_gate, out_up = refs[8:10]
    for i in range(8):
        place = slice_of(t[0], i % 4, i >= 4)
        at = pl.ds(pl.multiple_of(place * COLS, COLS), COLS)
        both = dot(xs[i][...], grads[...], TN).astype(BF)
        out_gate[at, :] = both[:, 0:HID]
        out_up[at, :] = both[:, HID : 2 * HID]


def weights_down_body(t, hidden, own, sib, out, h_v, own_v, sib_v, ht_v, out_v, sems):
    copies = Copies(sems)
    h_in = copies.start(hidden, h_v)
    pairs = [(side, half) for side in range(2) for half in range(2)]
    g_in = []
    for side, half in pairs:
        cols = slice(half * 2 * COLS, (half + 1) * 2 * COLS)
        src, dst = ((own, own_v), (sib, sib_v))[side]
        g_in.append(copies.start(src.at[:, cols], dst.at[:, cols]))
    h_in.wait()
    ht_v[...] = h_v[...].T
    done = []
    for (side, half), started in zip(pairs, g_in):
        started.wait()
        cols = slice(half * 2 * COLS, (half + 1) * 2 * COLS)
        part = dot(ht_v[...], (own_v, sib_v)[side][:, cols]).astype(BF)
        for j in range(2):
            dy = half * 2 + j
            place = out_v.at[:, slice((side * 4 + dy) * COLS, (side * 4 + dy + 1) * COLS)]
            place[...] = part[:, lanes(j)]
            at = pl.ds(pl.multiple_of(slice_of(t[0], dy, side == 1) * COLS, 128), COLS)
            done.append(copies.start(place, out.at[:, at]))
    wait_all(done)


def selection(routes):
    first, second, slot = slot_masks(routes)
    hots = [one_hot(slot, e) for e in range(EXPERTS)]
    both = jnp.concatenate(hots, axis=0).astype(BF)
    parts = [
        jnp.concatenate(
            [hots[e] * jnp.where(m[e : e + 1, :], 1.0, 0.0) for e in range(EXPERTS)], axis=0
        ).astype(BF)
        for m in (first, second)
    ]
    return both, parts


def combine_far_body(routes, rows, out, prob_out):
    both, parts = selection(routes[...])
    half = EXPERTS * CAP
    total = dot(both, rows[0:half, 0:COLS], TN) + dot(both, rows[half : 2 * half, 0:COLS], TN)
    out[...] = total.astype(BF)
    lanes = rows[0:half, COLS : COLS + 128], rows[half : 2 * half, COLS : COLS + 128]
    for k in range(2):
        value = dot(lanes[0], parts[k], TN) + dot(lanes[1], parts[k], TN)
        prob_out[k : k + 1, :] = value[0:1, :] + value[1:2, :]
    prob_out[2:8, :] = jnp.zeros((6, TOK), F32)


def finish_body(routes, probs, rows, far, q0, q1, q2, q3, out, prob_out):
    both, _ = selection(routes[...])
    half = EXPERTS * CAP
    total = dot(both, rows[0:half, :], TN) + dot(both, rows[half : 2 * half, :], TN)
    out[...] = (total + far[...].astype(F32)).astype(BF)
    prob = q0[0:2, :] + q1[0:2, :] + q2[0:2, :] + q3[0:2, :]
    prob_out[...] = prob / probs[...]


def on_device(tokens, d_out, routes, probs, w_gate, w_up, w_down):
    wg, wu, wd = w_gate[0], w_up[0], w_down[0]
    t = lax.axis_index("tensor").astype(jnp.int32).reshape(1)
    routes_t = routes.T
    probs_t = probs.T.astype(F32)

    def from_y(x, dy):
        return lax.ppermute(
            x, "tensor", [(i, ((i // 2 - dy) % 4) * 2 + i % 2) for i in range(8)]
        )

    def from_sibling(x):
        return lax.ppermute(x, "tensor", [(i, i ^ 1) for i in range(8)])

    def exchange(x):
        got = lax.all_to_all(x, ("dp", "ctx"), split_axis=0, concat_axis=0, tiled=True)
        return got.reshape(ROWS, x.shape[2])

    def after(x, *others):
        return lax.optimization_barrier((x,) + others)[0]

    MB = 1 << 20
    wide = 4 * COLS
    with jax.named_scope("dispatch"):
        gs = [d_out] + [from_y(d_out, dy) for dy in (1, 2, 3)]
        send_x = call(dispatch_x_body, sds((16, CAP, COLS)), flops=10**8, nbytes=MB)(routes_t, tokens)
        x0 = exchange(send_x)
        send_g = call(dispatch_g_body, sds((16, CAP, wide)), flops=2 * 10**8, nbytes=4 * MB)(
            routes_t, probs_t, *gs
        )
    with jax.named_scope("gather"):
        xs = [x0] + [from_y(x0, dy) for dy in (1, 2, 3)]
        x0_sib = from_sibling(x0)
        xs = xs + [x0_sib] + [from_sibling(x) for x in xs[1:]]
        g_own = exchange(after(send_g, x0))
    with jax.named_scope("forward"):
        act, slope, hidden = plain_call(
            forward_body,
            t,
            xs + [wg, wu],
            [sds((ROWS, HID), F32), sds((ROWS, HID), F32), sds((ROWS, HID))],
            [((ROWS, 8 * COLS), BF), ((8 * COLS, HID), BF), ((8 * COLS, HID), BF)]
            + [((ROWS, HID), F32), ((ROWS, HID), F32), ((ROWS, HID), BF)],
            46,
            6_500_000_000,
            18 * MB,
        )
        g_own = after(g_own, hidden)
        g_sib = from_sibling(g_own)
    with jax.named_scope("backward"):
        (back,) = plain_call(
            back_own_body,
            t,
            [g_own, wd],
            [sds((ROWS, HID), F32)],
            [((ROWS, wide), BF), ((HID, wide), BF), ((ROWS, HID), F32)],
            12,
            1_600_000_000,
            7 * MB,
        )
        got = plain_call(
            back_body,
            t,
            [g_sib, back, act, slope, hidden, wd, wg, wu],
            [sds((ROWS, 2 * HID)), sds((ROWS, 128))] + [sds((ROWS, COLS))] * 4,
            [((ROWS, wide), BF)]
            + [((ROWS, HID), F32)] * 3
            + [((ROWS, HID), BF), ((HID, wide), BF), ((wide, 2 * HID), BF)]
            + [((ROWS, 2 * HID), BF), ((ROWS, 128), BF), ((ROWS, wide), BF)],
            56,
            4_800_000_000,
            24 * MB,
        )
        grads, prob = got[:2]
        prob_sib = from_sibling(prob)
        part_sib = [from_sibling(p) for p in got[2:]]
    with jax.named_scope("weights_down"):
        (grad_down,) = plain_call(
            weights_down_body,
            t,
            [after(hidden, grads), g_own, g_sib],
            [sds((HID, 8 * COLS))],
            [((ROWS, HID), BF), ((ROWS, wide), BF), ((ROWS, wide), BF)]
            + [((HID, ROWS), BF), ((HID, 8 * COLS), BF)],
            13,
            3_300_000_000,
            10 * MB,
        )
    with jax.named_scope("sums"):
        out1, out2, out3 = plain_call(
            sums_body,
            t,
            [after(grads, grad_down), prob, prob_sib] + part_sib[1:] + [wg, wu],
            [sds((ROWS, COLS)), sds((ROWS, COLS + 128)), sds((ROWS, COLS))],
            [((ROWS, 2 * HID), BF), ((ROWS, 128), BF), ((ROWS, 128), BF)]
            + [((ROWS, COLS), BF)] * 3
            + [((3 * COLS, 2 * HID), BF)]
            + [((ROWS, COLS), BF), ((ROWS, COLS + 128), BF), ((ROWS, COLS), BF)],
            42,
            2_400_000_000,
            10 * MB,
        )
        left = from_y(out1, 3)
        right = from_y(out3, 1)
        far = exchange(out2.reshape(16, CAP, COLS + 128))
    vm = pl.BlockSpec(memory_space=pltpu.VMEM)
    sm = pl.BlockSpec(memory_space=pltpu.SMEM)
    with jax.named_scope("weights_gate_up"):
        grad_gate, grad_up = call(
            weights_gate_up_body,
            [sds((8 * COLS, HID))] * 2,
            flops=6_500_000_000,
            nbytes=15 * MB,
            in_specs=[sm] + [vm] * 9,
            out_specs=[vm] * 2,
        )(t, after(grads, out1, out2, out3), *xs)
    with jax.named_scope("last_sum"):
        (near,) = plain_call(
            last_sum_body,
            t,
            [after(grads, grad_gate), part_sib[0], left, right, wg, wu],
            [sds((ROWS, COLS))],
            [((ROWS, 2 * HID), BF)]
            + [((ROWS, COLS), BF)] * 3
            + [((COLS, 2 * HID), BF), ((ROWS, COLS), BF)],
            22,
            800_000_000,
            6 * MB,
        )
        near_rows = exchange(near.reshape(16, CAP, COLS))
    with jax.named_scope("finish"):
        far_part, prob_part = call(
            combine_far_body, [sds((TOK, COLS)), sds((8, TOK), F32)], flops=10**8, nbytes=MB
        )(routes_t, far)
        far_part = from_y(far_part, 2)
        probs_all = [prob_part] + [from_y(prob_part, dy) for dy in (1, 2, 3)]
        d_tokens, d_probs = call(
            finish_body, [sds((TOK, COLS)), sds((2, TOK), F32)], flops=10**8, nbytes=MB
        )(routes_t, probs_t, near_rows, far_part, *probs_all)
    return d_tokens, d_probs.T, grad_gate[None], grad_up[None], grad_down[None]


def solution(mesh):
    in_specs = (
        P(("dp", "ctx"), "tensor"),
        P(("dp", "ctx"), "tensor"),
        P(("dp", "ctx"), None),
        P(("dp", "ctx"), None),
        P("ctx", None, ("dp", "tensor")),
        P("ctx", None, ("dp", "tensor")),
        P("ctx", ("dp", "tensor"), None),
    )
    out_specs = (
        P(("dp", "ctx"), "tensor"),
        P(("dp", "ctx"), None),
        P("ctx", None, ("dp", "tensor")),
        P("ctx", None, ("dp", "tensor")),
        P("ctx", ("dp", "tensor"), None),
    )
    return jax.shard_map(
        on_device, mesh=mesh, in_specs=in_specs, out_specs=out_specs, check_vma=False
    )
```

```python
import jax
import jax.numpy as jnp
from jax import lax
from jax.experimental import pallas as pl
from jax.experimental.pallas import tpu as pltpu
from jax.sharding import PartitionSpec as P

BF = jnp.bfloat16
F32 = jnp.float32
VMEM_LIMIT = 56 * 1024 * 1024
EXPERTS = 8
CAP = 64
EARLY = 32
TOK = 128
COLS = 384
ROWS = 1024
HID = 512
NT = (((1,), (1,)), ((), ()))
TN = (((0,), (0,)), ((), ()))


def dot(a, b, dims=(((1,), (0,)), ((), ()))):
    return lax.dot_general(a, b, dims, preferred_element_type=F32)


def call(body, outs, grid=None, scratch=(), flops=0, nbytes=0, **specs):
    params = dict(vmem_limit_bytes=VMEM_LIMIT)
    return pl.pallas_call(
        body,
        out_shape=outs,
        compiler_params=pltpu.CompilerParams(**params),
        cost_estimate=pl.CostEstimate(flops=flops, bytes_accessed=nbytes, transcendentals=0),
        **specs,
    )


def sds(shape, dtype=BF):
    return jax.ShapeDtypeStruct(shape, dtype)


def slot_masks(routes):
    expert = lax.broadcasted_iota(jnp.int32, (EXPERTS, TOK), 0)
    first = routes[0:1, :] == expert
    second = routes[1:2, :] == expert
    named = jnp.where(first | second, 1.0, 0.0).astype(F32)
    before = lax.broadcasted_iota(jnp.int32, (TOK, TOK), 0)
    after = lax.broadcasted_iota(jnp.int32, (TOK, TOK), 1)
    earlier = jnp.where(before < after, 1.0, 0.0).astype(BF)
    rank = dot(named.astype(BF), earlier)
    slot = jnp.where(named > 0.0, rank, -1.0)
    return first, second, slot


def one_hot(slot, expert):
    place = lax.broadcasted_iota(jnp.int32, (CAP, TOK), 0).astype(F32)
    return jnp.where(slot[expert : expert + 1, :] == place, 1.0, 0.0)


def dispatch_x_body(routes, tokens, out):
    _, _, slot = slot_masks(routes[...])
    select = jnp.concatenate([one_hot(slot, e) for e in range(EXPERTS)], axis=0).astype(BF)
    rows = dot(select, tokens[...]).astype(BF).reshape(EXPERTS, CAP, COLS)
    out[0:EXPERTS] = rows
    out[EXPERTS : 2 * EXPERTS] = rows


def dispatch_g_body(routes, probs, g0, g1, g2, g3, out):
    first, _, slot = slot_masks(routes[...])
    p = probs[...].astype(F32)
    weight = jnp.where(first, p[0:1, :], p[1:2, :])
    select = jnp.concatenate(
        [one_hot(slot, e) * weight[e : e + 1, :] for e in range(EXPERTS)], axis=0
    ).astype(BF)
    for i, g in enumerate((g0, g1, g2, g3)):
        rows = dot(select, g[...]).astype(BF).reshape(EXPERTS, CAP, COLS)
        out[0:EXPERTS, :, i * COLS : (i + 1) * COLS] = rows
        out[EXPERTS : 2 * EXPERTS, :, i * COLS : (i + 1) * COLS] = rows


def slice_of(t, dy, sibling):
    core = t % 2
    core = 1 - core if sibling else core
    return ((t // 2 + dy) % 4) * 2 + core


def plain_call(body, t, ins, outs, scratch, copies, flops, nbytes):
    anywhere = pl.BlockSpec(memory_space=pltpu.HBM)
    return pl.pallas_call(
        body,
        out_shape=outs,
        in_specs=[pl.BlockSpec(memory_space=pltpu.SMEM)] + [anywhere] * len(ins),
        out_specs=[anywhere] * len(outs),
        scratch_shapes=[pltpu.VMEM(shape, dtype) for shape, dtype in scratch]
        + [pltpu.SemaphoreType.DMA((copies,))],
        compiler_params=pltpu.CompilerParams(vmem_limit_bytes=VMEM_LIMIT),
        cost_estimate=pl.CostEstimate(flops=flops, bytes_accessed=nbytes, transcendentals=0),
    )(t, *ins)


class Copies:
    def __init__(self, sems):
        self.sems, self.used = sems, 0

    def start(self, src, dst):
        copy = pltpu.make_async_copy(src, dst, self.sems.at[self.used])
        self.used += 1
        copy.start()
        return copy


def wait_all(copies):
    for copy in copies:
        copy.wait()


def slice_at(t, dy, sibling):
    return pl.ds(pl.multiple_of(slice_of(t[0], dy, sibling) * COLS, COLS), COLS)


def lanes(dy):
    return slice(dy * COLS, (dy + 1) * COLS)


def down_columns(copies, t, wd, into, sibling):
    return [
        copies.start(
            wd.at[:, pl.ds(pl.multiple_of(slice_of(t[0], dy, sibling) * COLS, 128), COLS)],
            into.at[:, lanes(dy)],
        )
        for dy in range(4)
    ]


def gate_up_rows(copies, t, wg, wu, into, steps, sibling):
    started = []
    for i, dy in enumerate(steps):
        at = slice_at(t, dy, sibling)
        started.append(copies.start(wg.at[at, :], into.at[lanes(i), 0:HID]))
        started.append(copies.start(wu.at[at, :], into.at[lanes(i), HID : 2 * HID]))
    return started


def chunks(rows):
    return [slice(r, r + rows) for r in range(0, ROWS, rows)]


def split_lanes(*values):
    lane = lax.broadcasted_iota(jnp.int32, values[0].shape[:-1] + (128,), values[0].ndim - 1)
    total = jnp.zeros(lane.shape, F32)
    for i, value in enumerate(values):
        upper = value.astype(BF).astype(F32)
        total = jnp.where(lane == 2 * i, upper, total)
        total = jnp.where(lane == 2 * i + 1, value - upper, total)
    return total.astype(BF)


def back_body(t, own, sib, act, slope, hidden, wd, wg, wu, grads, prob, *refs):
    parts = refs[:4]
    own_v, sib_v, act_v, slope_v, hidden_v, wd_o, wd_s, w_v, grads_v, prob_v, part_v, sems = refs[4:]
    copies = Copies(sems)
    pairs = ((own, own_v), (sib, sib_v), (act, act_v), (slope, slope_v), (hidden, hidden_v))
    rows = chunks(256)
    wd_in = down_columns(copies, t, wd, wd_o, False)
    ins = [[copies.start(a.at[rows[0]], b.at[rows[0]]) for a, b in pairs]]
    wd_in += down_columns(copies, t, wd, wd_s, True)
    w_in = gate_up_rows(copies, t, wg, wu, w_v, range(4), True)
    ins += [[copies.start(a.at[c], b.at[c]) for a, b in pairs] for c in rows[1:]]
    done = []
    for i, c in enumerate(rows):
        wait_all(ins[i])
        if i == 0:
            wait_all(wd_in[:4])
        back = dot(own_v[c], wd_o[...], NT)
        if i == 0:
            wait_all(wd_in[4:])
        back += dot(sib_v[c], wd_s[...], NT)
        prob_v[c] = split_lanes(
            jnp.sum(hidden_v[c].astype(F32) * back, axis=1, keepdims=True)
        )
        grads_v[c, 0:HID] = (back * slope_v[c]).astype(BF)
        grads_v[c, HID : 2 * HID] = (back * act_v[c]).astype(BF)
        if i == 0:
            wait_all(w_in)
        part_v[c] = dot(grads_v[c], w_v[...], NT).astype(BF)
        done.append(copies.start(grads_v.at[c], grads.at[c]))
        done.append(copies.start(prob_v.at[c], prob.at[c]))
        for dy in range(4):
            done.append(copies.start(part_v.at[c, lanes(dy)], parts[dy].at[c]))
    wait_all(done)


def sums_body(t, grads, prob, prob_sib, s0, s1, s2, s3, wg, wu, early, *refs):
    late, (grads_v, prob_v, sib_v) = refs[:4], refs[4:7]
    s_v, w_v, early_v, late_v, sems = refs[7:]
    copies = Copies(sems)
    w_in = gate_up_rows(copies, t, wg, wu, w_v, range(4), False)
    rows = chunks(256)
    ins = [
        [copies.start(a.at[c], b.at[c]) for a, b in ((grads, grads_v), (prob, prob_v), (prob_sib, sib_v))]
        + [copies.start(s.at[c], s_v.at[dy, c]) for dy, s in enumerate((s0, s1, s2, s3))]
        for c in rows
    ]
    wait_all(w_in)
    done = []
    for i, (c, started) in enumerate(zip(rows, ins)):
        wait_all(started)
        blocks = slice(i * 256 // CAP, (i + 1) * 256 // CAP)
        part = dot(grads_v[c], w_v[...], NT)
        for dy in range(4):
            value = (part[:, lanes(dy)] + s_v[dy, c].astype(F32)).astype(BF)
            value = value.reshape(256 // CAP, CAP, COLS)
            early_v[blocks, :, lanes(dy)] = value[:, 0:EARLY]
            late_v[dy, blocks] = value[:, EARLY:CAP]
        both = prob_v[c].astype(F32) + sib_v[c].astype(F32)
        both = jnp.sum(both, axis=1, keepdims=True).reshape(256 // CAP, CAP, 1)
        early_v[blocks, :, 4 * COLS : 4 * COLS + 128] = split_lanes(
            both[:, 0:EARLY], both[:, EARLY:CAP]
        )
        done.append(copies.start(early_v.at[blocks], early.at[blocks]))
        for dy in range(4):
            done.append(copies.start(late_v.at[dy, blocks], late[dy].at[blocks]))
    wait_all(done)


HALF = ROWS // 2


def part_of(source, c):
    if len(source) == 1:
        return source[0].at[c]
    half = c.start // HALF
    return source[half].at[slice(c.start - half * HALF, c.stop - half * HALF)]


def in_chunks(copies, sources, x_v, c):
    return [copies.start(part_of(x, c), x_v.at[c, lanes(i)]) for i, x in enumerate(sources)]


def near_forward_body(t, *refs):
    xs, wg, wu, out = [(x,) for x in refs[:6]], refs[6], refs[7], refs[8]
    x_v, w_v, out_v, sems = refs[9:]
    copies = Copies(sems)
    w_in = gate_up_rows(copies, t, wg, wu, w_v.at[0 : 3 * COLS], (0, 1, 3), False)
    w_in += gate_up_rows(copies, t, wg, wu, w_v.at[3 * COLS : 6 * COLS], (0, 1, 3), True)
    rows = chunks(256)
    ins = [in_chunks(copies, xs, x_v, c) for c in rows]
    wait_all(w_in)
    done = []
    for i, c in enumerate(rows):
        wait_all(ins[i])
        out_v[c] = dot(x_v[c], w_v[...])
        done.append(copies.start(out_v.at[c], out.at[c]))
    wait_all(done)


def forward_body(t, *refs):
    xs, near, wg, wu = [refs[0:2], refs[2:4]], *refs[4:7]
    act, slope, hidden, x_v, w_v, near_v, act_v, slope_v, hidden_v, sems = refs[7:]
    copies = Copies(sems)
    w_in = gate_up_rows(copies, t, wg, wu, w_v.at[0:COLS], (2,), False)
    w_in += gate_up_rows(copies, t, wg, wu, w_v.at[COLS : 2 * COLS], (2,), True)
    rows = chunks(256)
    ins = [
        in_chunks(copies, xs, x_v, c) + [copies.start(near.at[c], near_v.at[c])] for c in rows
    ]
    wait_all(w_in)
    done = []
    for i, c in enumerate(rows):
        wait_all(ins[i])
        total = near_v[c] + dot(x_v[c], w_v[...])
        gate, up = total[:, 0:HID], total[:, HID : 2 * HID]
        sigma = jax.nn.sigmoid(gate)
        active = gate * sigma
        act_v[c] = active
        slope_v[c] = up * (sigma * (1.0 + gate * (1.0 - sigma)))
        hidden_v[c] = (active * up).astype(BF)
        for a, b in ((act_v, act), (slope_v, slope), (hidden_v, hidden)):
            done.append(copies.start(a.at[c], b.at[c]))
    wait_all(done)


def weights_gate_up_body(t, grads, *refs):
    xs = [(0, 0, refs[0:1]), (1, 0, refs[1:2]), (3, 0, refs[2:3])]
    xs += [(0, 1, refs[3:4]), (1, 1, refs[4:5]), (3, 1, refs[5:6])]
    xs += [(2, 0, refs[6:8]), (2, 1, refs[8:10])]
    out_gate, out_up, grads_v, x_v, gate_v, up_v, sems = refs[10:]
    copies = Copies(sems)

    def load(i):
        parts = xs[i][2]
        rows = ROWS // len(parts)
        return [
            copies.start(p, x_v.at[i, h * rows : (h + 1) * rows]) for h, p in enumerate(parts)
        ]

    ins = [load(0)]
    grads_in = copies.start(grads, grads_v)
    ins += [load(i) for i in range(1, 8)]
    grads_in.wait()
    done = []
    for i, (dy, sibling, _) in enumerate(xs):
        wait_all(ins[i])
        both = dot(x_v[i], grads_v[...], TN).astype(BF)
        gate_v[lanes(i)] = both[:, 0:HID]
        up_v[lanes(i)] = both[:, HID : 2 * HID]
        at = slice_at(t, dy, sibling == 1)
        done.append(copies.start(gate_v.at[lanes(i)], out_gate.at[at]))
        done.append(copies.start(up_v.at[lanes(i)], out_up.at[at]))
    wait_all(done)


def weights_down_body(t, hidden, own, sib, out, h_v, own_v, sib_v, ht_v, out_v, sems):
    copies = Copies(sems)
    h_in = copies.start(hidden, h_v)
    pairs = [(side, half) for side in range(2) for half in range(2)]
    g_in = []
    for side, half in pairs:
        cols = slice(half * 2 * COLS, (half + 1) * 2 * COLS)
        src, dst = ((own, own_v), (sib, sib_v))[side]
        g_in.append(copies.start(src.at[:, cols], dst.at[:, cols]))
    h_in.wait()
    ht_v[...] = h_v[...].T
    done = []
    for (side, half), started in zip(pairs, g_in):
        started.wait()
        cols = slice(half * 2 * COLS, (half + 1) * 2 * COLS)
        part = dot(ht_v[...], (own_v, sib_v)[side][:, cols]).astype(BF)
        for j in range(2):
            dy = half * 2 + j
            place = out_v.at[:, slice((side * 4 + dy) * COLS, (side * 4 + dy + 1) * COLS)]
            place[...] = part[:, lanes(j)]
            at = pl.ds(pl.multiple_of(slice_of(t[0], dy, side == 1) * COLS, 128), COLS)
            done.append(copies.start(place, out.at[:, at]))
    wait_all(done)


def selection(routes):
    first, second, slot = slot_masks(routes)
    hots = [one_hot(slot, e) for e in range(EXPERTS)]
    kinds = [hots]
    for mask in (first, second):
        kinds.append([hots[e] * jnp.where(mask[e : e + 1, :], 1.0, 0.0) for e in range(EXPERTS)])
    return [
        [jnp.concatenate([h[at] for h in kind], axis=0).astype(BF) for kind in kinds]
        for at in (slice(0, EARLY), slice(EARLY, CAP))
    ]


def from_slots(select, rows, cols):
    half = EXPERTS * EARLY
    return dot(select, rows[0:half, cols], TN) + dot(select, rows[half : 2 * half, cols], TN)


def combine_body(routes, rows, own, own_lanes, m1, m2, m3):
    early, late = selection(routes[...])
    total = from_slots(early[0], rows, slice(0, 4 * COLS))
    own[...] = total[:, 0:COLS]
    at = slice(4 * COLS, 4 * COLS + 128)
    probs = []
    for k in (1, 2):
        a, b = from_slots(early[k], rows, at), from_slots(late[k], rows, at)
        probs.append(a[:, 0:1] + a[:, 1:2] + b[:, 2:3] + b[:, 3:4])
    prob_lanes = split_lanes(*probs)
    own_lanes[...] = prob_lanes
    for dy, m in ((1, m1), (2, m2), (3, m3)):
        m[:, 0:COLS] = total[:, lanes(dy)].astype(BF)
        m[:, COLS : COLS + 128] = prob_lanes


def finish_body(routes, probs, rows, own, own_lanes, m1, m2, m3, out, prob_out):
    _, late = selection(routes[...])
    total = from_slots(late[0], rows, slice(0, COLS)) + own[...]
    prob_lanes = own_lanes[...].astype(F32)
    for m in (m1, m2, m3):
        total += m[:, 0:COLS].astype(F32)
        prob_lanes += m[:, COLS : COLS + 128].astype(F32)
    out[...] = total.astype(BF)
    turned = prob_lanes.T
    p = probs[...].astype(F32)
    prob_out[0:1, :] = (turned[0:1, :] + turned[1:2, :]) / p[0:1, :]
    prob_out[1:2, :] = (turned[2:3, :] + turned[3:4, :]) / p[1:2, :]


def on_device(tokens, d_out, routes, probs, w_gate, w_up, w_down):
    wg, wu, wd = w_gate[0], w_up[0], w_down[0]
    t = lax.axis_index("tensor").astype(jnp.int32).reshape(1)
    routes_t = routes.T
    probs_t = probs.T

    def from_y(x, dy):
        return lax.ppermute(
            x, "tensor", [(i, ((i // 2 - dy) % 4) * 2 + i % 2) for i in range(8)]
        )

    def from_sibling(x):
        return lax.ppermute(x, "tensor", [(i, i ^ 1) for i in range(8)])

    def exchange(x):
        got = lax.all_to_all(x, ("dp", "ctx"), split_axis=0, concat_axis=0, tiled=True)
        return got.reshape(16 * x.shape[1], x.shape[2])

    def after(x, *others):
        return lax.optimization_barrier((x,) + others)[0]

    MB = 1 << 20
    wide = 4 * COLS
    with jax.named_scope("dispatch"):
        gs = [d_out] + [from_y(d_out, dy) for dy in (1, 2, 3)]
        send_x = call(dispatch_x_body, sds((16, CAP, COLS)), flops=10**8, nbytes=MB)(routes_t, tokens)
        x0 = exchange(send_x)
        send_g = call(dispatch_g_body, sds((16, CAP, wide)), flops=2 * 10**8, nbytes=4 * MB)(
            routes_t, probs_t, *gs
        )
    with jax.named_scope("gather"):
        up1, down1 = from_y(x0, 1), from_y(x0, 3)
        near_xs = [x0, up1, down1]
        near_xs += [from_sibling(x) for x in near_xs]
        far_xs = [from_y(down1[:HALF], 3), from_y(up1[HALF:], 1)]
        g_got = exchange(after(send_g, x0))
    with jax.named_scope("forward"):
        (near,) = plain_call(
            near_forward_body,
            t,
            near_xs + [wg, wu],
            [sds((ROWS, 2 * HID), F32)],
            [((ROWS, 6 * COLS), BF), ((6 * COLS, 2 * HID), BF), ((ROWS, 2 * HID), F32)],
            40,
            1,
            1,
        )
        far_xs += [from_sibling(after(x, near)) for x in far_xs]
        g_own = after(g_got, *far_xs)
        g_sib = from_sibling(g_own)
        act, slope, hidden = plain_call(
            forward_body,
            t,
            far_xs + [near, wg, wu],
            [sds((ROWS, HID), F32), sds((ROWS, HID), F32), sds((ROWS, HID))],
            [((ROWS, 2 * COLS), BF), ((2 * COLS, 2 * HID), BF), ((ROWS, 2 * HID), F32)]
            + [((ROWS, HID), F32), ((ROWS, HID), F32), ((ROWS, HID), BF)],
            28,
            1,
            1,
        )
    with jax.named_scope("backward"):
        got = plain_call(
            back_body,
            t,
            [g_own, g_sib, act, slope, hidden, wd, wg, wu],
            [sds((ROWS, 2 * HID)), sds((ROWS, 128))] + [sds((ROWS, COLS))] * 4,
            [((ROWS, wide), BF)] * 2
            + [((ROWS, HID), F32)] * 2
            + [((ROWS, HID), BF), ((HID, wide), BF), ((HID, wide), BF), ((wide, 2 * HID), BF)]
            + [((ROWS, 2 * HID), BF), ((ROWS, 128), BF), ((ROWS, wide), BF)],
            60,
            1,
            1,
        )
        grads, prob = got[:2]
        prob_sib = from_sibling(prob)
        part_sib = [from_sibling(p) for p in got[2:]]
    with jax.named_scope("sums"):
        sums = plain_call(
            sums_body,
            t,
            [grads, prob, prob_sib] + part_sib + [wg, wu],
            [sds((16, EARLY, wide + 128))] + [sds((16, CAP - EARLY, COLS))] * 4,
            [((ROWS, 2 * HID), BF), ((ROWS, 128), BF), ((ROWS, 128), BF)]
            + [((4, ROWS, COLS), BF), ((wide, 2 * HID), BF), ((16, EARLY, wide + 128), BF)]
            + [((4, 16, CAP - EARLY, COLS), BF)],
            56,
            1,
            1,
        )
        early, late = sums[0], sums[1:]
        arrived = [from_y(late[dy], 4 - dy) for dy in (1, 2, 3)]
        early_rows = exchange(early)
    with jax.named_scope("weights_gate_up"):
        grad_gate, grad_up = plain_call(
            weights_gate_up_body,
            t,
            [after(grads, early)] + near_xs + far_xs,
            [sds((8 * COLS, HID))] * 2,
            [((ROWS, 2 * HID), BF), ((8, ROWS, COLS), BF)] + [((8 * COLS, HID), BF)] * 2,
            27,
            1,
            1,
        )
    with jax.named_scope("weights_down"):
        (grad_down,) = plain_call(
            weights_down_body,
            t,
            [after(hidden, grad_gate), g_own, g_sib],
            [sds((HID, 8 * COLS))],
            [((ROWS, HID), BF), ((ROWS, wide), BF), ((ROWS, wide), BF)]
            + [((HID, ROWS), BF), ((HID, 8 * COLS), BF)],
            13,
            1,
            1,
        )
    with jax.named_scope("late_sum"):
        mine = after(late[0], grad_down)
        late_sum = sum((x.astype(F32) for x in arrived), mine.astype(F32)).astype(BF)
        late_rows = exchange(late_sum)
    with jax.named_scope("finish"):
        own, own_lanes, m1, m2, m3 = call(
            combine_body,
            [sds((TOK, COLS), F32), sds((TOK, 128))] + [sds((TOK, COLS + 128))] * 3,
            flops=1,
            nbytes=1,
        )(routes_t, early_rows)
        d_tokens, d_probs = call(
            finish_body, [sds((TOK, COLS)), sds((2, TOK), F32)], flops=1, nbytes=1
        )(
            routes_t,
            probs_t,
            late_rows,
            own,
            own_lanes,
            from_y(m1, 3),
            from_y(m2, 2),
            from_y(m3, 1),
        )
    return d_tokens, d_probs.T, grad_gate[None], grad_up[None], grad_down[None]


def solution(mesh):
    in_specs = (
        P(("dp", "ctx"), "tensor"),
        P(("dp", "ctx"), "tensor"),
        P(("dp", "ctx"), None),
        P(("dp", "ctx"), None),
        P("ctx", None, ("dp", "tensor")),
        P("ctx", None, ("dp", "tensor")),
        P("ctx", ("dp", "tensor"), None),
    )
    out_specs = (
        P(("dp", "ctx"), "tensor"),
        P(("dp", "ctx"), None),
        P("ctx", None, ("dp", "tensor")),
        P("ctx", None, ("dp", "tensor")),
        P("ctx", ("dp", "tensor"), None),
    )
    return jax.shard_map(
        on_device, mesh=mesh, in_specs=in_specs, out_specs=out_specs, check_vma=False
    )
```

```python
import jax
import jax.numpy as jnp
from jax import lax
from jax.experimental import pallas as pl
from jax.experimental.pallas import tpu as pltpu
from jax.sharding import PartitionSpec as P

BF = jnp.bfloat16
F32 = jnp.float32
VMEM_LIMIT = 62 * 1024 * 1024
EXPERTS = 8
CAP = 64
EARLY = 32
TOK = 128
COLS = 384
ROWS = 1024
HID = 512
NT = (((1,), (1,)), ((), ()))
TN = (((0,), (0,)), ((), ()))


def dot(a, b, dims=(((1,), (0,)), ((), ()))):
    return lax.dot_general(a, b, dims, preferred_element_type=F32)


def call(body, outs, grid=None, scratch=(), flops=0, nbytes=0, **specs):
    params = dict(vmem_limit_bytes=VMEM_LIMIT)
    return pl.pallas_call(
        body,
        out_shape=outs,
        compiler_params=pltpu.CompilerParams(**params),
        cost_estimate=pl.CostEstimate(flops=flops, bytes_accessed=nbytes, transcendentals=0),
        **specs,
    )


def sds(shape, dtype=BF):
    return jax.ShapeDtypeStruct(shape, dtype)


def slot_masks(routes):
    expert = lax.broadcasted_iota(jnp.int32, (EXPERTS, TOK), 0)
    first = routes[0:1, :] == expert
    second = routes[1:2, :] == expert
    named = jnp.where(first | second, 1.0, 0.0).astype(F32)
    before = lax.broadcasted_iota(jnp.int32, (TOK, TOK), 0)
    after = lax.broadcasted_iota(jnp.int32, (TOK, TOK), 1)
    earlier = jnp.where(before < after, 1.0, 0.0).astype(BF)
    rank = dot(named.astype(BF), earlier)
    slot = jnp.where(named > 0.0, rank, -1.0)
    return first, second, slot


def one_hot(slot, expert):
    place = lax.broadcasted_iota(jnp.int32, (CAP, TOK), 0).astype(F32)
    return jnp.where(slot[expert : expert + 1, :] == place, 1.0, 0.0)


def dispatch_x_body(routes, tokens, out):
    _, _, slot = slot_masks(routes[...])
    select = jnp.concatenate([one_hot(slot, e) for e in range(EXPERTS)], axis=0).astype(BF)
    rows = dot(select, tokens[...]).astype(BF).reshape(EXPERTS, CAP, COLS)
    out[0:EXPERTS] = rows
    out[EXPERTS : 2 * EXPERTS] = rows


def dispatch_g_body(routes, probs, g0, g1, g2, g3, out):
    first, _, slot = slot_masks(routes[...])
    p = probs[...].astype(F32)
    weight = jnp.where(first, p[0:1, :], p[1:2, :])
    select = jnp.concatenate(
        [one_hot(slot, e) * weight[e : e + 1, :] for e in range(EXPERTS)], axis=0
    ).astype(BF)
    for i, g in enumerate((g0, g1, g2, g3)):
        rows = dot(select, g[...]).astype(BF).reshape(EXPERTS, CAP, COLS)
        out[0:EXPERTS, :, i * COLS : (i + 1) * COLS] = rows
        out[EXPERTS : 2 * EXPERTS, :, i * COLS : (i + 1) * COLS] = rows


def slice_of(t, dy, sibling):
    core = t % 2
    core = 1 - core if sibling else core
    return ((t // 2 + dy) % 4) * 2 + core


def plain_call(body, t, ins, outs, scratch, copies, flops, nbytes):
    anywhere = pl.BlockSpec(memory_space=pltpu.HBM)
    return pl.pallas_call(
        body,
        out_shape=outs,
        in_specs=[pl.BlockSpec(memory_space=pltpu.SMEM)] + [anywhere] * len(ins),
        out_specs=[anywhere] * len(outs),
        scratch_shapes=[pltpu.VMEM(shape, dtype) for shape, dtype in scratch]
        + [pltpu.SemaphoreType.DMA((copies,))],
        compiler_params=pltpu.CompilerParams(vmem_limit_bytes=VMEM_LIMIT),
        cost_estimate=pl.CostEstimate(flops=flops, bytes_accessed=nbytes, transcendentals=0),
    )(t, *ins)


class Copies:
    def __init__(self, sems):
        self.sems, self.used = sems, 0

    def start(self, src, dst):
        copy = pltpu.make_async_copy(src, dst, self.sems.at[self.used])
        self.used += 1
        copy.start()
        return copy


def wait_all(copies):
    for copy in copies:
        copy.wait()


def slice_at(t, dy, sibling):
    return pl.ds(pl.multiple_of(slice_of(t[0], dy, sibling) * COLS, COLS), COLS)


def lanes(dy):
    return slice(dy * COLS, (dy + 1) * COLS)


def down_columns(copies, t, wd, into, sibling):
    return [
        copies.start(
            wd.at[:, pl.ds(pl.multiple_of(slice_of(t[0], dy, sibling) * COLS, 128), COLS)],
            into.at[:, lanes(dy)],
        )
        for dy in range(4)
    ]


def gate_up_rows(copies, t, wg, wu, into, steps, sibling):
    started = []
    for i, dy in enumerate(steps):
        at = slice_at(t, dy, sibling)
        started.append(copies.start(wg.at[at, :], into.at[lanes(i), 0:HID]))
        started.append(copies.start(wu.at[at, :], into.at[lanes(i), HID : 2 * HID]))
    return started


def chunks(rows):
    return [slice(r, r + rows) for r in range(0, ROWS, rows)]


def split_lanes(*values):
    lane = lax.broadcasted_iota(jnp.int32, values[0].shape[:-1] + (128,), values[0].ndim - 1)
    total = jnp.zeros(lane.shape, F32)
    for i, value in enumerate(values):
        upper = value.astype(BF).astype(F32)
        total = jnp.where(lane == 2 * i, upper, total)
        total = jnp.where(lane == 2 * i + 1, value - upper, total)
    return total.astype(BF)


def back_body(t, own, sib, act, slope, hidden, wd, grads, prob, *refs):
    own_v, sib_v, act_v, slope_v, hidden_v, wd_o, wd_s, grads_v, prob_v, sems = refs
    copies = Copies(sems)
    pairs = ((own, own_v), (sib, sib_v), (act, act_v), (slope, slope_v), (hidden, hidden_v))
    rows = chunks(256)
    wd_in = down_columns(copies, t, wd, wd_o, False)
    ins = [[copies.start(a.at[rows[0]], b.at[rows[0]]) for a, b in pairs]]
    wd_in += down_columns(copies, t, wd, wd_s, True)
    ins += [[copies.start(a.at[c], b.at[c]) for a, b in pairs] for c in rows[1:]]
    done = []
    for i, c in enumerate(rows):
        wait_all(ins[i])
        if i == 0:
            wait_all(wd_in[:4])
        back = dot(own_v[c], wd_o[...], NT)
        if i == 0:
            wait_all(wd_in[4:])
        back += dot(sib_v[c], wd_s[...], NT)
        prob_v[c] = split_lanes(
            jnp.sum(hidden_v[c].astype(F32) * back, axis=1, keepdims=True)
        )
        grads_v[c, 0:HID] = (back * slope_v[c]).astype(BF)
        grads_v[c, HID : 2 * HID] = (back * act_v[c]).astype(BF)
        done.append(copies.start(grads_v.at[c], grads.at[c]))
        done.append(copies.start(prob_v.at[c], prob.at[c]))
    wait_all(done)


STEP = 4


def own_part_body(t, grads, wg, wu, out, g_v, w_v, out_v, sems):
    copies = Copies(sems)
    rows = chunks(256)
    ins = [copies.start(grads.at[rows[0]], g_v.at[rows[0]])]
    w_in = gate_up_rows(copies, t, wg, wu, w_v, range(4), False)
    ins += [copies.start(grads.at[c], g_v.at[c]) for c in rows[1:]]
    wait_all(w_in)
    done = []
    for c, started in zip(rows, ins):
        started.wait()
        out_v[c] = dot(g_v[c], w_v[...], NT).astype(BF)
        done.append(copies.start(out_v.at[c], out.at[c]))
    wait_all(done)


def sums_body(t, own, grads_sib, prob, prob_sib, sib_wg, sib_wu, early, *refs):
    late, (own_v, g_v, p_v, q_v, w_v, early_v, late_v, sems) = refs[:4], refs[4:]
    copies = Copies(sems)
    blocks = [slice(i, i + STEP) for i in range(0, 16, STEP)]
    pairs = ((grads_sib, g_v), (own, own_v), (prob, p_v), (prob_sib, q_v))
    ins = [[copies.start(x.at[blocks[0]], v.at[blocks[0]]) for x, v in pairs]]
    w_in = []
    for dy in range(4):
        y = (t[0] // 2 + dy) % 4
        w_in.append(copies.start(sib_wg.at[y], w_v.at[lanes(dy), 0:HID]))
        w_in.append(copies.start(sib_wu.at[y], w_v.at[lanes(dy), HID : 2 * HID]))
    ins += [[copies.start(x.at[b], v.at[b]) for x, v in pairs] for b in blocks[1:]]
    wait_all(w_in)
    done = []
    for b, started in zip(blocks, ins):
        wait_all(started)
        part = dot(g_v[b].reshape(STEP * CAP, 2 * HID), w_v[...], NT)
        for dy in range(4):
            value = part[:, lanes(dy)].reshape(STEP, CAP, COLS)
            value = (value + own_v[b, :, lanes(dy)].astype(F32)).astype(BF)
            early_v[b, :, lanes(dy)] = value[:, 0:EARLY]
            late_v[dy, b] = value[:, EARLY:CAP]
        both = p_v[b].astype(F32) + q_v[b].astype(F32)
        both = jnp.sum(both, axis=2, keepdims=True)
        early_v[b, :, 4 * COLS : 4 * COLS + 128] = split_lanes(
            both[:, 0:EARLY], both[:, EARLY:CAP]
        )
        done.append(copies.start(early_v.at[b], early.at[b]))
        for dy in range(4):
            done.append(copies.start(late_v.at[dy, b], late[dy].at[b]))
    wait_all(done)


HALF = ROWS // 2


def part_of(source, c):
    if len(source) == 1:
        return source[0].at[c]
    half = c.start // HALF
    return source[half].at[slice(c.start - half * HALF, c.stop - half * HALF)]


def in_chunks(copies, sources, x_v, c):
    return [copies.start(part_of(x, c), x_v.at[c, lanes(i)]) for i, x in enumerate(sources)]


def near_forward_body(t, *refs):
    xs, wg, wu, out = [(x,) for x in refs[:6]], refs[6], refs[7], refs[8]
    x_v, w_v, out_v, sems = refs[9:]
    copies = Copies(sems)
    w_in = gate_up_rows(copies, t, wg, wu, w_v.at[0 : 3 * COLS], (0, 1, 3), False)
    w_in += gate_up_rows(copies, t, wg, wu, w_v.at[3 * COLS : 6 * COLS], (0, 1, 3), True)
    rows = chunks(256)
    ins = [in_chunks(copies, xs, x_v, c) for c in rows]
    wait_all(w_in)
    done = []
    for i, c in enumerate(rows):
        wait_all(ins[i])
        out_v[c] = dot(x_v[c], w_v[...])
        done.append(copies.start(out_v.at[c], out.at[c]))
    wait_all(done)


def forward_body(t, *refs):
    xs, near, wg, wu = [refs[0:2], refs[2:4]], *refs[4:7]
    act, slope, hidden, x_v, w_v, near_v, act_v, slope_v, hidden_v, sems = refs[7:]
    copies = Copies(sems)
    w_in = gate_up_rows(copies, t, wg, wu, w_v.at[0:COLS], (2,), False)
    w_in += gate_up_rows(copies, t, wg, wu, w_v.at[COLS : 2 * COLS], (2,), True)
    rows = chunks(256)
    ins = [
        in_chunks(copies, xs, x_v, c) + [copies.start(near.at[c], near_v.at[c])] for c in rows
    ]
    wait_all(w_in)
    done = []
    for i, c in enumerate(rows):
        wait_all(ins[i])
        total = near_v[c] + dot(x_v[c], w_v[...])
        gate, up = total[:, 0:HID], total[:, HID : 2 * HID]
        sigma = jax.nn.sigmoid(gate)
        active = gate * sigma
        act_v[c] = active
        slope_v[c] = up * (sigma * (1.0 + gate * (1.0 - sigma)))
        hidden_v[c] = (active * up).astype(BF)
        for a, b in ((act_v, act), (slope_v, slope), (hidden_v, hidden)):
            done.append(copies.start(a.at[c], b.at[c]))
    wait_all(done)


def weights_gate_up_body(t, grads, *refs):
    xs = [(0, 0, refs[0:1]), (1, 0, refs[1:2]), (3, 0, refs[2:3])]
    xs += [(0, 1, refs[3:4]), (1, 1, refs[4:5]), (3, 1, refs[5:6])]
    xs += [(2, 0, refs[6:8]), (2, 1, refs[8:10])]
    out_gate, out_up, grads_v, x_v, gate_v, up_v, sems = refs[10:]
    copies = Copies(sems)

    def load(i):
        parts = xs[i][2]
        rows = ROWS // len(parts)
        return [
            copies.start(p, x_v.at[i, h * rows : (h + 1) * rows]) for h, p in enumerate(parts)
        ]

    ins = [load(0)]
    grads_in = copies.start(grads, grads_v)
    ins += [load(i) for i in range(1, 8)]
    grads_in.wait()
    done = []
    for i, (dy, sibling, _) in enumerate(xs):
        wait_all(ins[i])
        both = dot(x_v[i], grads_v[...], TN).astype(BF)
        gate_v[lanes(i)] = both[:, 0:HID]
        up_v[lanes(i)] = both[:, HID : 2 * HID]
        at = slice_at(t, dy, sibling == 1)
        done.append(copies.start(gate_v.at[lanes(i)], out_gate.at[at]))
        done.append(copies.start(up_v.at[lanes(i)], out_up.at[at]))
    wait_all(done)


def weights_down_body(t, hidden, own, sib, out, h_v, own_v, sib_v, ht_v, out_v, sems):
    copies = Copies(sems)
    h_in = copies.start(hidden, h_v)
    pairs = [(side, half) for side in range(2) for half in range(2)]
    g_in = []
    for side, half in pairs:
        cols = slice(half * 2 * COLS, (half + 1) * 2 * COLS)
        src, dst = ((own, own_v), (sib, sib_v))[side]
        g_in.append(copies.start(src.at[:, cols], dst.at[:, cols]))
    h_in.wait()
    ht_v[...] = h_v[...].T
    done = []
    for (side, half), started in zip(pairs, g_in):
        started.wait()
        cols = slice(half * 2 * COLS, (half + 1) * 2 * COLS)
        part = dot(ht_v[...], (own_v, sib_v)[side][:, cols]).astype(BF)
        for j in range(2):
            dy = half * 2 + j
            place = out_v.at[:, slice((side * 4 + dy) * COLS, (side * 4 + dy + 1) * COLS)]
            place[...] = part[:, lanes(j)]
            at = pl.ds(pl.multiple_of(slice_of(t[0], dy, side == 1) * COLS, 128), COLS)
            done.append(copies.start(place, out.at[:, at]))
    wait_all(done)


def selection(masks, at, choice=None):
    first, second, slot = masks
    hots = [one_hot(slot, e) for e in range(EXPERTS)]
    if choice is not None:
        mask = (first, second)[choice]
        hots = [hots[e] * jnp.where(mask[e : e + 1, :], 1.0, 0.0) for e in range(EXPERTS)]
    return jnp.concatenate([h[at] for h in hots], axis=0).astype(BF)


EARLY_SLOTS, LATE_SLOTS = slice(0, EARLY), slice(EARLY, CAP)


def from_slots(select, rows, cols):
    half = EXPERTS * EARLY
    return dot(select, rows[0:half, cols], TN) + dot(select, rows[half : 2 * half, cols], TN)


def combine_body(routes, rows, own, own_lanes, m1, m2, m3):
    masks = slot_masks(routes[...])
    total = from_slots(selection(masks, EARLY_SLOTS), rows, slice(0, 4 * COLS))
    own[...] = total[:, 0:COLS]
    at = slice(4 * COLS, 4 * COLS + 128)
    probs = []
    for k in range(2):
        a = from_slots(selection(masks, EARLY_SLOTS, k), rows, at)
        b = from_slots(selection(masks, LATE_SLOTS, k), rows, at)
        probs.append(a[:, 0:1] + a[:, 1:2] + b[:, 2:3] + b[:, 3:4])
    prob_lanes = split_lanes(*probs)
    own_lanes[...] = prob_lanes
    for dy, m in ((1, m1), (2, m2), (3, m3)):
        m[:, 0:COLS] = total[:, lanes(dy)].astype(BF)
        m[:, COLS : COLS + 128] = prob_lanes


def finish_body(routes, probs, rows, own, own_lanes, m1, m2, m3, out, prob_out):
    late = selection(slot_masks(routes[...]), LATE_SLOTS)
    total = from_slots(late, rows, slice(0, COLS)) + own[...]
    prob_lanes = own_lanes[...].astype(F32)
    for m in (m1, m2, m3):
        total += m[:, 0:COLS].astype(F32)
        prob_lanes += m[:, COLS : COLS + 128].astype(F32)
    out[...] = total.astype(BF)
    turned = prob_lanes.T
    p = probs[...].astype(F32)
    prob_out[0:1, :] = (turned[0:1, :] + turned[1:2, :]) / p[0:1, :]
    prob_out[1:2, :] = (turned[2:3, :] + turned[3:4, :]) / p[1:2, :]


def on_device(tokens, d_out, routes, probs, w_gate, w_up, w_down):
    wg, wu, wd = w_gate[0], w_up[0], w_down[0]
    t = lax.axis_index("tensor").astype(jnp.int32).reshape(1)
    routes_t = routes.T
    probs_t = probs.T

    def from_y(x, dy):
        return lax.ppermute(
            x, "tensor", [(i, ((i // 2 - dy) % 4) * 2 + i % 2) for i in range(8)]
        )

    def from_sibling(x):
        return lax.ppermute(x, "tensor", [(i, i ^ 1) for i in range(8)])

    def exchange(x):
        got = lax.all_to_all(x, ("dp", "ctx"), split_axis=0, concat_axis=0, tiled=True)
        return got.reshape(16 * x.shape[1], x.shape[2])

    def after(x, *others):
        return lax.optimization_barrier((x,) + others)[0]

    MB = 1 << 20
    wide = 4 * COLS
    with jax.named_scope("dispatch"):
        gs = [d_out] + [from_y(d_out, dy) for dy in (1, 2, 3)]
        send_x = call(dispatch_x_body, sds((16, CAP, COLS)), flops=10**8, nbytes=MB)(routes_t, tokens)
        x0 = exchange(send_x)
        send_g = call(dispatch_g_body, sds((16, CAP, wide)), flops=2 * 10**8, nbytes=4 * MB)(
            routes_t, probs_t, *gs
        )
    with jax.named_scope("gather"):
        up1, down1 = from_y(x0, 1), from_y(x0, 3)
        near_xs = [x0, up1, down1]
        near_xs += [from_sibling(x) for x in near_xs]
        far_xs = [from_y(down1[:HALF], 3), from_y(up1[HALF:], 1)]
        g_got = exchange(after(send_g, x0))
        core = t[0] % 2

        def sibling_rows(w):
            its = lax.dynamic_index_in_dim(w.reshape(4, 2, COLS, HID), 1 - core, 1, False)
            return from_sibling(after(its, x0))

        sib_wg, sib_wu = sibling_rows(wg), sibling_rows(wu)
    with jax.named_scope("forward"):
        (near,) = plain_call(
            near_forward_body,
            t,
            near_xs + [wg, wu],
            [sds((ROWS, 2 * HID), F32)],
            [((ROWS, 6 * COLS), BF), ((6 * COLS, 2 * HID), BF), ((ROWS, 2 * HID), F32)],
            40,
            1,
            1,
        )
        far_xs += [from_sibling(after(x, near)) for x in far_xs]
        g_own = after(g_got, sib_wg, sib_wu, *far_xs)
        g_sib = from_sibling(g_own)
        act, slope, hidden = plain_call(
            forward_body,
            t,
            far_xs + [near, wg, wu],
            [sds((ROWS, HID), F32), sds((ROWS, HID), F32), sds((ROWS, HID))],
            [((ROWS, 2 * COLS), BF), ((2 * COLS, 2 * HID), BF), ((ROWS, 2 * HID), F32)]
            + [((ROWS, HID), F32), ((ROWS, HID), F32), ((ROWS, HID), BF)],
            28,
            1,
            1,
        )
    with jax.named_scope("backward"):
        grads, prob = plain_call(
            back_body,
            t,
            [g_own, g_sib, act, slope, hidden, wd],
            [sds((ROWS, 2 * HID)), sds((ROWS, 128))],
            [((ROWS, wide), BF)] * 2
            + [((ROWS, HID), F32)] * 2
            + [((ROWS, HID), BF), ((HID, wide), BF), ((HID, wide), BF)]
            + [((ROWS, 2 * HID), BF), ((ROWS, 128), BF)],
            36,
            1,
            1,
        )
        grads_sib, prob_sib = from_sibling(grads), from_sibling(prob)

    def blocks(x):
        return x.reshape(16, CAP, x.shape[1])

    with jax.named_scope("sums"):
        (own_part,) = plain_call(
            own_part_body,
            t,
            [grads, wg, wu],
            [sds((ROWS, wide))],
            [((ROWS, 2 * HID), BF), ((wide, 2 * HID), BF), ((ROWS, wide), BF)],
            16,
            1,
            1,
        )
        early, *late = plain_call(
            sums_body,
            t,
            [blocks(x) for x in (own_part, grads_sib, prob, prob_sib)] + [sib_wg, sib_wu],
            [sds((16, EARLY, wide + 128))] + [sds((16, CAP - EARLY, COLS))] * 4,
            [((16, CAP, wide), BF), ((16, CAP, 2 * HID), BF)]
            + [((16, CAP, 128), BF), ((16, CAP, 128), BF)]
            + [((wide, 2 * HID), BF), ((16, EARLY, wide + 128), BF)]
            + [((4, 16, CAP - EARLY, COLS), BF)],
            44,
            1,
            1,
        )
        early_rows = exchange(early)
        arrived = [from_y(late[dy], 4 - dy) for dy in (1, 2, 3)]
    with jax.named_scope("weights_gate_up"):
        grad_gate, grad_up = plain_call(
            weights_gate_up_body,
            t,
            [after(grads, late[0])] + near_xs + far_xs,
            [sds((8 * COLS, HID))] * 2,
            [((ROWS, 2 * HID), BF), ((8, ROWS, COLS), BF)] + [((8 * COLS, HID), BF)] * 2,
            27,
            1,
            1,
        )
    with jax.named_scope("weights_down"):
        (grad_down,) = plain_call(
            weights_down_body,
            t,
            [after(hidden, grad_gate), g_own, g_sib],
            [sds((HID, 8 * COLS))],
            [((ROWS, HID), BF), ((ROWS, wide), BF), ((ROWS, wide), BF)]
            + [((HID, ROWS), BF), ((HID, 8 * COLS), BF)],
            13,
            1,
            1,
        )
    with jax.named_scope("late_sum"):
        mine = after(late[0], grad_down)
        late_sum = sum((x.astype(F32) for x in arrived), mine.astype(F32)).astype(BF)
        late_rows = exchange(late_sum)
    with jax.named_scope("finish"):
        own, own_lanes, m1, m2, m3 = call(
            combine_body,
            [sds((TOK, COLS), F32), sds((TOK, 128))] + [sds((TOK, COLS + 128))] * 3,
            flops=1,
            nbytes=1,
        )(routes_t, early_rows)
        d_tokens, d_probs = call(
            finish_body, [sds((TOK, COLS)), sds((2, TOK), F32)], flops=1, nbytes=1
        )(
            routes_t,
            probs_t,
            late_rows,
            own,
            own_lanes,
            from_y(m1, 3),
            from_y(m2, 2),
            from_y(m3, 1),
        )
    return d_tokens, d_probs.T, grad_gate[None], grad_up[None], grad_down[None]


def solution(mesh):
    in_specs = (
        P(("dp", "ctx"), "tensor"),
        P(("dp", "ctx"), "tensor"),
        P(("dp", "ctx"), None),
        P(("dp", "ctx"), None),
        P("ctx", None, ("dp", "tensor")),
        P("ctx", None, ("dp", "tensor")),
        P("ctx", ("dp", "tensor"), None),
    )
    out_specs = (
        P(("dp", "ctx"), "tensor"),
        P(("dp", "ctx"), None),
        P("ctx", None, ("dp", "tensor")),
        P("ctx", None, ("dp", "tensor")),
        P("ctx", ("dp", "tensor"), None),
    )
    return jax.shard_map(
        on_device, mesh=mesh, in_specs=in_specs, out_specs=out_specs, check_vma=False
    )
```

```python
import jax
import jax.numpy as jnp
from jax import lax
from jax.experimental import pallas as pl
from jax.experimental.pallas import tpu as pltpu
from jax.sharding import PartitionSpec as P

BF = jnp.bfloat16
F32 = jnp.float32
VMEM_LIMIT = 62 * 1024 * 1024
SMALL_LIMIT = 16 * 1024 * 1024
EXPERTS = 8
CAP = 64
EARLY = 32
TOK = 128
COLS = 384
ROWS = 1024
HID = 512
NT = (((1,), (1,)), ((), ()))
TN = (((0,), (0,)), ((), ()))


def dot(a, b, dims=(((1,), (0,)), ((), ()))):
    return lax.dot_general(a, b, dims, preferred_element_type=F32)


def call(body, outs, limit, flops=0, nbytes=0):
    return pl.pallas_call(
        body,
        out_shape=outs,
        compiler_params=pltpu.CompilerParams(vmem_limit_bytes=limit),
        cost_estimate=pl.CostEstimate(flops=flops, bytes_accessed=nbytes, transcendentals=0),
    )


def sds(shape, dtype=BF):
    return jax.ShapeDtypeStruct(shape, dtype)


def slot_masks(routes):
    expert = lax.broadcasted_iota(jnp.int32, (EXPERTS, TOK), 0)
    first = routes[0:1, :] == expert
    second = routes[1:2, :] == expert
    named = jnp.where(first | second, 1.0, 0.0).astype(F32)
    before = lax.broadcasted_iota(jnp.int32, (TOK, TOK), 0)
    after = lax.broadcasted_iota(jnp.int32, (TOK, TOK), 1)
    earlier = jnp.where(before < after, 1.0, 0.0).astype(BF)
    rank = dot(named.astype(BF), earlier)
    slot = jnp.where(named > 0.0, rank, -1.0)
    return first, second, slot


def one_hot(slot, expert):
    place = lax.broadcasted_iota(jnp.int32, (CAP, TOK), 0).astype(F32)
    return jnp.where(slot[expert : expert + 1, :] == place, 1.0, 0.0)


def dispatch_x_body(routes, tokens, out):
    _, _, slot = slot_masks(routes[...])
    select = jnp.concatenate([one_hot(slot, e) for e in range(EXPERTS)], axis=0).astype(BF)
    rows = dot(select, tokens[...]).astype(BF).reshape(EXPERTS, CAP, COLS)
    out[0:EXPERTS] = rows
    out[EXPERTS : 2 * EXPERTS] = rows


def dispatch_g_body(routes, probs, g0, g1, g2, g3, out):
    first, _, slot = slot_masks(routes[...])
    p = probs[...].astype(F32)
    weight = jnp.where(first, p[0:1, :], p[1:2, :])
    select = jnp.concatenate(
        [one_hot(slot, e) * weight[e : e + 1, :] for e in range(EXPERTS)], axis=0
    ).astype(BF)
    for i, g in enumerate((g0, g1, g2, g3)):
        rows = dot(select, g[...]).astype(BF).reshape(EXPERTS, CAP, COLS)
        out[0:EXPERTS, :, i * COLS : (i + 1) * COLS] = rows
        out[EXPERTS : 2 * EXPERTS, :, i * COLS : (i + 1) * COLS] = rows


def slice_of(t, dy, sibling):
    core = t % 2
    core = 1 - core if sibling else core
    return ((t // 2 + dy) % 4) * 2 + core


def plain_call(body, t, ins, outs, scratch, copies, flops, nbytes):
    anywhere = pl.BlockSpec(memory_space=pltpu.HBM)
    return pl.pallas_call(
        body,
        out_shape=outs,
        in_specs=[pl.BlockSpec(memory_space=pltpu.SMEM)] + [anywhere] * len(ins),
        out_specs=[anywhere] * len(outs),
        scratch_shapes=[pltpu.VMEM(shape, dtype) for shape, dtype in scratch]
        + [pltpu.SemaphoreType.DMA((copies,))],
        compiler_params=pltpu.CompilerParams(vmem_limit_bytes=VMEM_LIMIT),
        cost_estimate=pl.CostEstimate(flops=flops, bytes_accessed=nbytes, transcendentals=0),
    )(t, *ins)


class Copies:
    def __init__(self, sems):
        self.sems, self.used = sems, 0

    def start(self, src, dst):
        copy = pltpu.make_async_copy(src, dst, self.sems.at[self.used])
        self.used += 1
        copy.start()
        return copy


def wait_all(copies):
    for copy in copies:
        copy.wait()


def slice_at(t, dy, sibling):
    return pl.ds(pl.multiple_of(slice_of(t[0], dy, sibling) * COLS, COLS), COLS)


def lanes(dy):
    return slice(dy * COLS, (dy + 1) * COLS)


def down_columns(copies, t, wd, into, sibling):
    return [
        copies.start(
            wd.at[:, pl.ds(pl.multiple_of(slice_of(t[0], dy, sibling) * COLS, 128), COLS)],
            into.at[:, lanes(dy)],
        )
        for dy in range(4)
    ]


def gate_up_rows(copies, t, wg, wu, into, steps, sibling):
    started = []
    for i, dy in enumerate(steps):
        at = slice_at(t, dy, sibling)
        started.append(copies.start(wg.at[at, :], into.at[lanes(i), 0:HID]))
        started.append(copies.start(wu.at[at, :], into.at[lanes(i), HID : 2 * HID]))
    return started


def chunks(rows):
    return [slice(r, r + rows) for r in range(0, ROWS, rows)]


def split_lanes(*values):
    lane = lax.broadcasted_iota(jnp.int32, values[0].shape[:-1] + (128,), values[0].ndim - 1)
    total = jnp.zeros(lane.shape, F32)
    for i, value in enumerate(values):
        upper = value.astype(BF).astype(F32)
        total = jnp.where(lane == 2 * i, upper, total)
        total = jnp.where(lane == 2 * i + 1, value - upper, total)
    return total.astype(BF)


def back_body(t, own, sib, act, slope, hidden, wd, grads, prob, *refs):
    own_v, sib_v, act_v, slope_v, hidden_v, wd_o, wd_s, grads_v, prob_v, sems = refs
    copies = Copies(sems)
    pairs = ((own, own_v), (sib, sib_v), (act, act_v), (slope, slope_v), (hidden, hidden_v))
    rows = chunks(256)
    wd_in = down_columns(copies, t, wd, wd_o, False)
    ins = [[copies.start(a.at[rows[0]], b.at[rows[0]]) for a, b in pairs]]
    wd_in += down_columns(copies, t, wd, wd_s, True)
    ins += [[copies.start(a.at[c], b.at[c]) for a, b in pairs] for c in rows[1:]]
    done = []
    for i, c in enumerate(rows):
        wait_all(ins[i])
        if i == 0:
            wait_all(wd_in[:4])
        back = dot(own_v[c], wd_o[...], NT)
        if i == 0:
            wait_all(wd_in[4:])
        back += dot(sib_v[c], wd_s[...], NT)
        prob_v[c] = split_lanes(
            jnp.sum(hidden_v[c].astype(F32) * back, axis=1, keepdims=True)
        )
        grads_v[c, 0:HID] = (back * slope_v[c]).astype(BF)
        grads_v[c, HID : 2 * HID] = (back * act_v[c]).astype(BF)
        done.append(copies.start(grads_v.at[c], grads.at[c]))
        done.append(copies.start(prob_v.at[c], prob.at[c]))
    wait_all(done)


STEP = 4


def own_part_body(t, grads, wg, wu, out, g_v, w_v, out_v, sems):
    copies = Copies(sems)
    rows = chunks(256)
    ins = [copies.start(grads.at[rows[0]], g_v.at[rows[0]])]
    w_in = gate_up_rows(copies, t, wg, wu, w_v, range(4), False)
    ins += [copies.start(grads.at[c], g_v.at[c]) for c in rows[1:]]
    wait_all(w_in)
    done = []
    for c, started in zip(rows, ins):
        started.wait()
        out_v[c] = dot(g_v[c], w_v[...], NT).astype(BF)
        done.append(copies.start(out_v.at[c], out.at[c]))
    wait_all(done)


def sums_body(t, own, grads_sib, prob, prob_sib, sib_wg, sib_wu, early, *refs):
    late, (own_v, g_v, p_v, q_v, w_v, early_v, late_v, sems) = refs[:4], refs[4:]
    copies = Copies(sems)
    blocks = [slice(i, i + STEP) for i in range(0, 16, STEP)]
    pairs = ((grads_sib, g_v), (own, own_v), (prob, p_v), (prob_sib, q_v))
    ins = [[copies.start(x.at[blocks[0]], v.at[blocks[0]]) for x, v in pairs]]
    w_in = []
    for dy in range(4):
        y = (t[0] // 2 + dy) % 4
        w_in.append(copies.start(sib_wg.at[y], w_v.at[lanes(dy), 0:HID]))
        w_in.append(copies.start(sib_wu.at[y], w_v.at[lanes(dy), HID : 2 * HID]))
    ins += [[copies.start(x.at[b], v.at[b]) for x, v in pairs] for b in blocks[1:]]
    wait_all(w_in)
    done = []
    for b, started in zip(blocks, ins):
        wait_all(started)
        part = dot(g_v[b].reshape(STEP * CAP, 2 * HID), w_v[...], NT)
        for dy in range(4):
            value = part[:, lanes(dy)].reshape(STEP, CAP, COLS)
            value = (value + own_v[b, :, lanes(dy)].astype(F32)).astype(BF)
            early_v[b, :, lanes(dy)] = value[:, 0:EARLY]
            late_v[dy, b] = value[:, EARLY:CAP]
        both = p_v[b].astype(F32) + q_v[b].astype(F32)
        both = jnp.sum(both, axis=2, keepdims=True)
        early_v[b, :, 4 * COLS : 4 * COLS + 128] = split_lanes(
            both[:, 0:EARLY], both[:, EARLY:CAP]
        )
        done.append(copies.start(early_v.at[b], early.at[b]))
        for dy in range(4):
            done.append(copies.start(late_v.at[dy, b], late[dy].at[b]))
    wait_all(done)


HALF = ROWS // 2


def part_of(source, c):
    if len(source) == 1:
        return source[0].at[c]
    half = c.start // HALF
    return source[half].at[slice(c.start - half * HALF, c.stop - half * HALF)]


def in_chunks(copies, sources, x_v, c):
    return [copies.start(part_of(x, c), x_v.at[c, lanes(i)]) for i, x in enumerate(sources)]


def near_forward_body(t, *refs):
    xs, wg, wu, out = [(x,) for x in refs[:6]], refs[6], refs[7], refs[8]
    x_v, w_v, out_v, sems = refs[9:]
    copies = Copies(sems)
    w_in = gate_up_rows(copies, t, wg, wu, w_v.at[0 : 3 * COLS], (0, 1, 3), False)
    w_in += gate_up_rows(copies, t, wg, wu, w_v.at[3 * COLS : 6 * COLS], (0, 1, 3), True)
    rows = chunks(256)
    ins = [in_chunks(copies, xs, x_v, c) for c in rows]
    wait_all(w_in)
    done = []
    for i, c in enumerate(rows):
        wait_all(ins[i])
        out_v[c] = dot(x_v[c], w_v[...])
        done.append(copies.start(out_v.at[c], out.at[c]))
    wait_all(done)


def forward_body(t, *refs):
    xs, near, wg, wu = [refs[0:2], refs[2:4]], *refs[4:7]
    act, slope, hidden, x_v, w_v, near_v, act_v, slope_v, hidden_v, sems = refs[7:]
    copies = Copies(sems)
    w_in = gate_up_rows(copies, t, wg, wu, w_v.at[0:COLS], (2,), False)
    w_in += gate_up_rows(copies, t, wg, wu, w_v.at[COLS : 2 * COLS], (2,), True)
    rows = chunks(256)
    ins = [
        in_chunks(copies, xs, x_v, c) + [copies.start(near.at[c], near_v.at[c])] for c in rows
    ]
    wait_all(w_in)
    done = []
    for i, c in enumerate(rows):
        wait_all(ins[i])
        total = near_v[c] + dot(x_v[c], w_v[...])
        gate, up = total[:, 0:HID], total[:, HID : 2 * HID]
        sigma = jax.nn.sigmoid(gate)
        active = gate * sigma
        act_v[c] = active
        slope_v[c] = up * (sigma * (1.0 + gate * (1.0 - sigma)))
        hidden_v[c] = (active * up).astype(BF)
        for a, b in ((act_v, act), (slope_v, slope), (hidden_v, hidden)):
            done.append(copies.start(a.at[c], b.at[c]))
    wait_all(done)


def weights_gate_up_body(t, grads, *refs):
    xs = [(0, 0, refs[0:1]), (1, 0, refs[1:2]), (3, 0, refs[2:3])]
    xs += [(0, 1, refs[3:4]), (1, 1, refs[4:5]), (3, 1, refs[5:6])]
    xs += [(2, 0, refs[6:8]), (2, 1, refs[8:10])]
    out_gate, out_up, grads_v, x_v, gate_v, up_v, sems = refs[10:]
    copies = Copies(sems)

    def load(i):
        parts = xs[i][2]
        rows = ROWS // len(parts)
        return [
            copies.start(p, x_v.at[i, h * rows : (h + 1) * rows]) for h, p in enumerate(parts)
        ]

    ins = [load(0)]
    grads_in = copies.start(grads, grads_v)
    ins += [load(i) for i in range(1, 8)]
    grads_in.wait()
    done = []
    for i, (dy, sibling, _) in enumerate(xs):
        wait_all(ins[i])
        both = dot(x_v[i], grads_v[...], TN).astype(BF)
        gate_v[lanes(i)] = both[:, 0:HID]
        up_v[lanes(i)] = both[:, HID : 2 * HID]
        at = slice_at(t, dy, sibling == 1)
        done.append(copies.start(gate_v.at[lanes(i)], out_gate.at[at]))
        done.append(copies.start(up_v.at[lanes(i)], out_up.at[at]))
    wait_all(done)


def weights_down_body(t, hidden, own, sib, out, h_v, own_v, sib_v, ht_v, out_v, sems):
    copies = Copies(sems)
    h_in = copies.start(hidden, h_v)
    pairs = [(side, half) for side in range(2) for half in range(2)]
    g_in = []
    for side, half in pairs:
        cols = slice(half * 2 * COLS, (half + 1) * 2 * COLS)
        src, dst = ((own, own_v), (sib, sib_v))[side]
        g_in.append(copies.start(src.at[:, cols], dst.at[:, cols]))
    h_in.wait()
    ht_v[...] = h_v[...].T
    done = []
    for (side, half), started in zip(pairs, g_in):
        started.wait()
        cols = slice(half * 2 * COLS, (half + 1) * 2 * COLS)
        part = dot(ht_v[...], (own_v, sib_v)[side][:, cols]).astype(BF)
        for j in range(2):
            dy = half * 2 + j
            place = out_v.at[:, slice((side * 4 + dy) * COLS, (side * 4 + dy + 1) * COLS)]
            place[...] = part[:, lanes(j)]
            at = pl.ds(pl.multiple_of(slice_of(t[0], dy, side == 1) * COLS, 128), COLS)
            done.append(copies.start(place, out.at[:, at]))
    wait_all(done)


def selection(masks, at, choice=None):
    first, second, slot = masks
    hots = [one_hot(slot, e) for e in range(EXPERTS)]
    if choice is not None:
        mask = (first, second)[choice]
        hots = [hots[e] * jnp.where(mask[e : e + 1, :], 1.0, 0.0) for e in range(EXPERTS)]
    return jnp.concatenate([h[at] for h in hots], axis=0).astype(BF)


EARLY_SLOTS, LATE_SLOTS = slice(0, EARLY), slice(EARLY, CAP)


def from_slots(select, rows, cols):
    half = EXPERTS * EARLY
    return dot(select, rows[0:half, cols], TN) + dot(select, rows[half : 2 * half, cols], TN)


def combine_body(routes, rows, own, own_lanes, m1, m2, m3):
    masks = slot_masks(routes[...])
    total = from_slots(selection(masks, EARLY_SLOTS), rows, slice(0, 4 * COLS))
    own[...] = total[:, 0:COLS]
    at = slice(4 * COLS, 4 * COLS + 128)
    probs = []
    for k in range(2):
        a = from_slots(selection(masks, EARLY_SLOTS, k), rows, at)
        b = from_slots(selection(masks, LATE_SLOTS, k), rows, at)
        probs.append(a[:, 0:1] + a[:, 1:2] + b[:, 2:3] + b[:, 3:4])
    prob_lanes = split_lanes(*probs)
    own_lanes[...] = prob_lanes
    for dy, m in ((1, m1), (2, m2), (3, m3)):
        m[:, 0:COLS] = total[:, lanes(dy)].astype(BF)
        m[:, COLS : COLS + 128] = prob_lanes


def finish_body(routes, probs, rows, own, own_lanes, m1, m2, m3, out, prob_out):
    late = selection(slot_masks(routes[...]), LATE_SLOTS)
    total = from_slots(late, rows, slice(0, COLS)) + own[...]
    prob_lanes = own_lanes[...].astype(F32)
    for m in (m1, m2, m3):
        total += m[:, 0:COLS].astype(F32)
        prob_lanes += m[:, COLS : COLS + 128].astype(F32)
    out[...] = total.astype(BF)
    turned = prob_lanes.T
    p = probs[...].astype(F32)
    prob_out[0:1, :] = (turned[0:1, :] + turned[1:2, :]) / p[0:1, :]
    prob_out[1:2, :] = (turned[2:3, :] + turned[3:4, :]) / p[1:2, :]


def on_device(tokens, d_out, routes, probs, w_gate, w_up, w_down):
    wg, wu, wd = w_gate[0], w_up[0], w_down[0]
    t = lax.axis_index("tensor").astype(jnp.int32).reshape(1)
    routes_t = routes.T
    probs_t = probs.T

    def from_y(x, dy):
        return lax.ppermute(
            x, "tensor", [(i, ((i // 2 - dy) % 4) * 2 + i % 2) for i in range(8)]
        )

    def from_sibling(x):
        return lax.ppermute(x, "tensor", [(i, i ^ 1) for i in range(8)])

    def exchange(x):
        got = lax.all_to_all(x, ("dp", "ctx"), split_axis=0, concat_axis=0, tiled=True)
        return got.reshape(16 * x.shape[1], x.shape[2])

    def after(x, *others):
        return lax.optimization_barrier((x,) + others)[0]

    MB = 1 << 20
    wide = 4 * COLS
    with jax.named_scope("dispatch"):
        gs = [d_out] + [from_y(d_out, dy) for dy in (1, 2, 3)]
        send_x = call(dispatch_x_body, sds((16, CAP, COLS)), VMEM_LIMIT, flops=10**8, nbytes=MB)(routes_t, tokens)
        x0 = exchange(send_x)
        send_g = call(dispatch_g_body, sds((16, CAP, wide)), VMEM_LIMIT, flops=2 * 10**8, nbytes=4 * MB)(
            routes_t, probs_t, *gs
        )
    with jax.named_scope("gather"):
        up1, down1 = from_y(x0, 1), from_y(x0, 3)
        near_xs = [x0, up1, down1]
        near_xs += [from_sibling(x) for x in near_xs]
        far_xs = [from_y(down1[:HALF], 3), from_y(up1[HALF:], 1)]
        g_got = exchange(after(send_g, x0))
        core = t[0] % 2

        def sibling_rows(w):
            its = lax.dynamic_index_in_dim(w.reshape(4, 2, COLS, HID), 1 - core, 1, False)
            return from_sibling(after(its, x0))

        sib_wg, sib_wu = sibling_rows(wg), sibling_rows(wu)
    with jax.named_scope("forward"):
        (near,) = plain_call(
            near_forward_body,
            t,
            near_xs + [wg, wu],
            [sds((ROWS, 2 * HID), F32)],
            [((ROWS, 6 * COLS), BF), ((6 * COLS, 2 * HID), BF), ((ROWS, 2 * HID), F32)],
            40,
            1,
            1,
        )
        far_xs += [from_sibling(after(x, near)) for x in far_xs]
        g_own = after(g_got, sib_wg, sib_wu, *far_xs)
        g_sib = from_sibling(g_own)
        act, slope, hidden = plain_call(
            forward_body,
            t,
            far_xs + [near, wg, wu],
            [sds((ROWS, HID), F32), sds((ROWS, HID), F32), sds((ROWS, HID))],
            [((ROWS, 2 * COLS), BF), ((2 * COLS, 2 * HID), BF), ((ROWS, 2 * HID), F32)]
            + [((ROWS, HID), F32), ((ROWS, HID), F32), ((ROWS, HID), BF)],
            28,
            1,
            1,
        )
    with jax.named_scope("backward"):
        grads, prob = plain_call(
            back_body,
            t,
            [g_own, g_sib, act, slope, hidden, wd],
            [sds((ROWS, 2 * HID)), sds((ROWS, 128))],
            [((ROWS, wide), BF)] * 2
            + [((ROWS, HID), F32)] * 2
            + [((ROWS, HID), BF), ((HID, wide), BF), ((HID, wide), BF)]
            + [((ROWS, 2 * HID), BF), ((ROWS, 128), BF)],
            36,
            1,
            1,
        )
        grads_sib, prob_sib = from_sibling(grads), from_sibling(prob)

    def blocks(x):
        return x.reshape(16, CAP, x.shape[1])

    with jax.named_scope("sums"):
        (own_part,) = plain_call(
            own_part_body,
            t,
            [grads, wg, wu],
            [sds((ROWS, wide))],
            [((ROWS, 2 * HID), BF), ((wide, 2 * HID), BF), ((ROWS, wide), BF)],
            16,
            1,
            1,
        )
        early, *late = plain_call(
            sums_body,
            t,
            [blocks(x) for x in (own_part, grads_sib, prob, prob_sib)] + [sib_wg, sib_wu],
            [sds((16, EARLY, wide + 128))] + [sds((16, CAP - EARLY, COLS))] * 4,
            [((16, CAP, wide), BF), ((16, CAP, 2 * HID), BF)]
            + [((16, CAP, 128), BF), ((16, CAP, 128), BF)]
            + [((wide, 2 * HID), BF), ((16, EARLY, wide + 128), BF)]
            + [((4, 16, CAP - EARLY, COLS), BF)],
            44,
            1,
            1,
        )
        early_rows = exchange(early)
        arrived = [from_y(late[dy], 4 - dy) for dy in (1, 2, 3)]
    with jax.named_scope("weights_gate_up"):
        grad_gate, grad_up = plain_call(
            weights_gate_up_body,
            t,
            [after(grads, late[0])] + near_xs + far_xs,
            [sds((8 * COLS, HID))] * 2,
            [((ROWS, 2 * HID), BF), ((8, ROWS, COLS), BF)] + [((8 * COLS, HID), BF)] * 2,
            27,
            1,
            1,
        )
    with jax.named_scope("weights_down"):
        (grad_down,) = plain_call(
            weights_down_body,
            t,
            [after(hidden, grad_gate), g_own, g_sib],
            [sds((HID, 8 * COLS))],
            [((ROWS, HID), BF), ((ROWS, wide), BF), ((ROWS, wide), BF)]
            + [((HID, ROWS), BF), ((HID, 8 * COLS), BF)],
            13,
            1,
            1,
        )
    with jax.named_scope("late_sum"):
        mine = after(late[0], grad_down)
        late_sum = sum((x.astype(F32) for x in arrived), mine.astype(F32)).astype(BF)
        late_rows = exchange(late_sum)
    with jax.named_scope("finish"):
        own, own_lanes, m1, m2, m3 = call(
            combine_body,
            [sds((TOK, COLS), F32), sds((TOK, 128))] + [sds((TOK, COLS + 128))] * 3,
            SMALL_LIMIT,
            flops=1,
            nbytes=1,
        )(routes_t, early_rows)
        d_tokens, d_probs = call(
            finish_body, [sds((TOK, COLS)), sds((2, TOK), F32)], SMALL_LIMIT, flops=1, nbytes=1
        )(
            routes_t,
            probs_t,
            late_rows,
            own,
            own_lanes,
            from_y(m1, 3),
            from_y(m2, 2),
            from_y(m3, 1),
        )
    return d_tokens, d_probs.T, grad_gate[None], grad_up[None], grad_down[None]


def solution(mesh):
    in_specs = (
        P(("dp", "ctx"), "tensor"),
        P(("dp", "ctx"), "tensor"),
        P(("dp", "ctx"), None),
        P(("dp", "ctx"), None),
        P("ctx", None, ("dp", "tensor")),
        P("ctx", None, ("dp", "tensor")),
        P("ctx", ("dp", "tensor"), None),
    )
    out_specs = (
        P(("dp", "ctx"), "tensor"),
        P(("dp", "ctx"), None),
        P("ctx", None, ("dp", "tensor")),
        P("ctx", None, ("dp", "tensor")),
        P("ctx", ("dp", "tensor"), None),
    )
    return jax.shard_map(
        on_device, mesh=mesh, in_specs=in_specs, out_specs=out_specs, check_vma=False
    )
```

```python
import jax
import jax.numpy as jnp
from jax import lax
from jax.experimental import pallas as pl
from jax.experimental.pallas import tpu as pltpu
from jax.sharding import PartitionSpec as P

BF = jnp.bfloat16
F32 = jnp.float32
VMEM_LIMIT = 62 * 1024 * 1024
SMALL_LIMIT = 16 * 1024 * 1024
EXPERTS = 8
CAP = 64
EARLY = 32
TOK = 128
COLS = 384
ROWS = 1024
HID = 512
NT = (((1,), (1,)), ((), ()))
TN = (((0,), (0,)), ((), ()))


def dot(a, b, dims=(((1,), (0,)), ((), ()))):
    return lax.dot_general(a, b, dims, preferred_element_type=F32)


def call(body, outs, limit, flops=0, nbytes=0):
    return pl.pallas_call(
        body,
        out_shape=outs,
        compiler_params=pltpu.CompilerParams(vmem_limit_bytes=limit),
        cost_estimate=pl.CostEstimate(flops=flops, bytes_accessed=nbytes, transcendentals=0),
    )


def sds(shape, dtype=BF):
    return jax.ShapeDtypeStruct(shape, dtype)


def slot_masks(routes):
    expert = lax.broadcasted_iota(jnp.int32, (EXPERTS, TOK), 0)
    first = routes[0:1, :] == expert
    second = routes[1:2, :] == expert
    named = jnp.where(first | second, 1.0, 0.0).astype(F32)
    before = lax.broadcasted_iota(jnp.int32, (TOK, TOK), 0)
    after = lax.broadcasted_iota(jnp.int32, (TOK, TOK), 1)
    earlier = jnp.where(before < after, 1.0, 0.0).astype(BF)
    rank = dot(named.astype(BF), earlier)
    slot = jnp.where(named > 0.0, rank, -1.0)
    return first, second, slot


def one_hot(slot, expert):
    place = lax.broadcasted_iota(jnp.int32, (CAP, TOK), 0).astype(F32)
    return jnp.where(slot[expert : expert + 1, :] == place, 1.0, 0.0)


def dispatch_x_body(routes, tokens, out):
    _, _, slot = slot_masks(routes[...])
    select = jnp.concatenate([one_hot(slot, e) for e in range(EXPERTS)], axis=0).astype(BF)
    rows = dot(select, tokens[...]).astype(BF).reshape(EXPERTS, CAP, COLS)
    out[0:EXPERTS] = rows
    out[EXPERTS : 2 * EXPERTS] = rows


def dispatch_g_body(routes, probs, g0, g1, g2, g3, out):
    first, _, slot = slot_masks(routes[...])
    p = probs[...].astype(F32)
    weight = jnp.where(first, p[0:1, :], p[1:2, :])
    select = jnp.concatenate(
        [one_hot(slot, e) * weight[e : e + 1, :] for e in range(EXPERTS)], axis=0
    ).astype(BF)
    for i, g in enumerate((g0, g1, g2, g3)):
        rows = dot(select, g[...]).astype(BF).reshape(EXPERTS, CAP, COLS)
        out[0:EXPERTS, :, i * COLS : (i + 1) * COLS] = rows
        out[EXPERTS : 2 * EXPERTS, :, i * COLS : (i + 1) * COLS] = rows


def slice_of(t, dy, sibling):
    core = t % 2
    core = 1 - core if sibling else core
    return ((t // 2 + dy) % 4) * 2 + core


def plain_call(body, t, ins, outs, scratch, copies, flops, nbytes):
    anywhere = pl.BlockSpec(memory_space=pltpu.HBM)
    return pl.pallas_call(
        body,
        out_shape=outs,
        in_specs=[pl.BlockSpec(memory_space=pltpu.SMEM)] + [anywhere] * len(ins),
        out_specs=[anywhere] * len(outs),
        scratch_shapes=[pltpu.VMEM(shape, dtype) for shape, dtype in scratch]
        + [pltpu.SemaphoreType.DMA((copies,))],
        compiler_params=pltpu.CompilerParams(vmem_limit_bytes=VMEM_LIMIT),
        cost_estimate=pl.CostEstimate(flops=flops, bytes_accessed=nbytes, transcendentals=0),
    )(t, *ins)


class Copies:
    def __init__(self, sems):
        self.sems, self.used = sems, 0

    def start(self, src, dst):
        copy = pltpu.make_async_copy(src, dst, self.sems.at[self.used])
        self.used += 1
        copy.start()
        return copy


def wait_all(copies):
    for copy in copies:
        copy.wait()


def slice_at(t, dy, sibling):
    return pl.ds(pl.multiple_of(slice_of(t[0], dy, sibling) * COLS, COLS), COLS)


def lanes(dy):
    return slice(dy * COLS, (dy + 1) * COLS)


def down_columns(copies, t, wd, into, sibling):
    return [
        copies.start(
            wd.at[:, pl.ds(pl.multiple_of(slice_of(t[0], dy, sibling) * COLS, 128), COLS)],
            into.at[:, lanes(dy)],
        )
        for dy in range(4)
    ]


def gate_up_rows(copies, t, wg, wu, into, steps, sibling):
    started = []
    for i, dy in enumerate(steps):
        at = slice_at(t, dy, sibling)
        started.append(copies.start(wg.at[at, :], into.at[lanes(i), 0:HID]))
        started.append(copies.start(wu.at[at, :], into.at[lanes(i), HID : 2 * HID]))
    return started


def chunks(rows):
    return [slice(r, r + rows) for r in range(0, ROWS, rows)]


def split_lanes(*values):
    lane = lax.broadcasted_iota(jnp.int32, values[0].shape[:-1] + (128,), values[0].ndim - 1)
    total = jnp.zeros(lane.shape, F32)
    for i, value in enumerate(values):
        upper = value.astype(BF).astype(F32)
        total = jnp.where(lane == 2 * i, upper, total)
        total = jnp.where(lane == 2 * i + 1, value - upper, total)
    return total.astype(BF)


def back_body(t, own, sib, act, slope, hidden, wd, grads, prob, *refs):
    own_v, sib_v, act_v, slope_v, hidden_v, wd_o, wd_s, grads_v, prob_v, sems = refs
    copies = Copies(sems)
    pairs = ((own, own_v), (sib, sib_v), (act, act_v), (slope, slope_v), (hidden, hidden_v))
    rows = chunks(256)
    wd_in = down_columns(copies, t, wd, wd_o, False)
    ins = [[copies.start(a.at[rows[0]], b.at[rows[0]]) for a, b in pairs]]
    wd_in += down_columns(copies, t, wd, wd_s, True)
    ins += [[copies.start(a.at[c], b.at[c]) for a, b in pairs] for c in rows[1:]]
    done = []
    for i, c in enumerate(rows):
        wait_all(ins[i])
        if i == 0:
            wait_all(wd_in[:4])
        back = dot(own_v[c], wd_o[...], NT)
        if i == 0:
            wait_all(wd_in[4:])
        back += dot(sib_v[c], wd_s[...], NT)
        prob_v[c] = split_lanes(
            jnp.sum(hidden_v[c].astype(F32) * back, axis=1, keepdims=True)
        )
        grads_v[c, 0:HID] = (back * slope_v[c]).astype(BF)
        grads_v[c, HID : 2 * HID] = (back * act_v[c]).astype(BF)
        done.append(copies.start(grads_v.at[c], grads.at[c]))
        done.append(copies.start(prob_v.at[c], prob.at[c]))
    wait_all(done)


STEP = 4


def own_part_body(t, grads, wg, wu, out, g_v, w_v, out_v, sems):
    copies = Copies(sems)
    rows = chunks(256)
    ins = [copies.start(grads.at[rows[0]], g_v.at[rows[0]])]
    w_in = gate_up_rows(copies, t, wg, wu, w_v, range(4), False)
    ins += [copies.start(grads.at[c], g_v.at[c]) for c in rows[1:]]
    done = []
    for i, (c, started) in enumerate(zip(rows, ins)):
        started.wait()
        for pair in (0, 2):
            if i == 0:
                wait_all(w_in[2 * pair : 2 * pair + 4])
            at = slice(pair * COLS, (pair + 2) * COLS)
            out_v[c, at] = dot(g_v[c], w_v[at], NT).astype(BF)
        done.append(copies.start(out_v.at[c], out.at[c]))
    wait_all(done)


def sums_body(t, own, grads_sib, prob, prob_sib, sib_wg, sib_wu, early, *refs):
    late, (own_v, g_v, p_v, q_v, w_v, early_v, late_v, sems) = refs[:4], refs[4:]
    copies = Copies(sems)
    blocks = [slice(i, i + STEP) for i in range(0, 16, STEP)]
    pairs = ((grads_sib, g_v), (own, own_v), (prob, p_v), (prob_sib, q_v))
    ins = [[copies.start(x.at[blocks[0]], v.at[blocks[0]]) for x, v in pairs]]
    w_in = []
    for dy in range(4):
        y = (t[0] // 2 + dy) % 4
        w_in.append(copies.start(sib_wg.at[y], w_v.at[lanes(dy), 0:HID]))
        w_in.append(copies.start(sib_wu.at[y], w_v.at[lanes(dy), HID : 2 * HID]))
    ins += [[copies.start(x.at[b], v.at[b]) for x, v in pairs] for b in blocks[1:]]
    done = []
    for i, (b, started) in enumerate(zip(blocks, ins)):
        wait_all(started)
        for pair in (0, 2):
            if i == 0:
                wait_all(w_in[2 * pair : 2 * pair + 4])
            at = slice(pair * COLS, (pair + 2) * COLS)
            part = dot(g_v[b].reshape(STEP * CAP, 2 * HID), w_v[at], NT)
            for dy in (pair, pair + 1):
                value = part[:, lanes(dy - pair)].reshape(STEP, CAP, COLS)
                value = (value + own_v[b, :, lanes(dy)].astype(F32)).astype(BF)
                early_v[b, :, lanes(dy)] = value[:, 0:EARLY]
                late_v[dy, b] = value[:, EARLY:CAP]
        both = p_v[b].astype(F32) + q_v[b].astype(F32)
        both = jnp.sum(both, axis=2, keepdims=True)
        early_v[b, :, 4 * COLS : 4 * COLS + 128] = split_lanes(
            both[:, 0:EARLY], both[:, EARLY:CAP]
        )
        done.append(copies.start(early_v.at[b], early.at[b]))
        for dy in range(4):
            done.append(copies.start(late_v.at[dy, b], late[dy].at[b]))
    wait_all(done)


HALF = ROWS // 2


def part_of(source, c):
    if len(source) == 1:
        return source[0].at[c]
    half = c.start // HALF
    return source[half].at[slice(c.start - half * HALF, c.stop - half * HALF)]


def in_chunks(copies, sources, x_v, c):
    return [copies.start(part_of(x, c), x_v.at[c, lanes(i)]) for i, x in enumerate(sources)]


def near_forward_body(t, *refs):
    xs, wg, wu, out = [(x,) for x in refs[:6]], refs[6], refs[7], refs[8]
    x_v, w_v, out_v, sems = refs[9:]
    copies = Copies(sems)
    w_in = gate_up_rows(copies, t, wg, wu, w_v.at[0 : 3 * COLS], (0, 1, 3), False)
    w_in += gate_up_rows(copies, t, wg, wu, w_v.at[3 * COLS : 6 * COLS], (0, 1, 3), True)
    rows = chunks(256)
    ins = [in_chunks(copies, xs, x_v, c) for c in rows]
    wait_all(w_in)
    done = []
    for i, c in enumerate(rows):
        wait_all(ins[i])
        out_v[c] = dot(x_v[c], w_v[...])
        done.append(copies.start(out_v.at[c], out.at[c]))
    wait_all(done)


def forward_body(t, *refs):
    xs, near, wg, wu = [refs[0:2], refs[2:4]], *refs[4:7]
    act, slope, hidden, x_v, w_v, near_v, act_v, slope_v, hidden_v, sems = refs[7:]
    copies = Copies(sems)
    w_in = gate_up_rows(copies, t, wg, wu, w_v.at[0:COLS], (2,), False)
    w_in += gate_up_rows(copies, t, wg, wu, w_v.at[COLS : 2 * COLS], (2,), True)
    rows = chunks(256)
    ins = [
        in_chunks(copies, xs, x_v, c) + [copies.start(near.at[c], near_v.at[c])] for c in rows
    ]
    wait_all(w_in)
    done = []
    for i, c in enumerate(rows):
        wait_all(ins[i])
        total = near_v[c] + dot(x_v[c], w_v[...])
        gate, up = total[:, 0:HID], total[:, HID : 2 * HID]
        sigma = jax.nn.sigmoid(gate)
        active = gate * sigma
        act_v[c] = active
        slope_v[c] = up * (sigma * (1.0 + gate * (1.0 - sigma)))
        hidden_v[c] = (active * up).astype(BF)
        for a, b in ((act_v, act), (slope_v, slope), (hidden_v, hidden)):
            done.append(copies.start(a.at[c], b.at[c]))
    wait_all(done)


def weights_gate_up_body(t, grads, *refs):
    xs = [(0, 0, refs[0:1]), (1, 0, refs[1:2]), (3, 0, refs[2:3])]
    xs += [(0, 1, refs[3:4]), (1, 1, refs[4:5]), (3, 1, refs[5:6])]
    xs += [(2, 0, refs[6:8]), (2, 1, refs[8:10])]
    out_gate, out_up, grads_v, x_v, gate_v, up_v, sems = refs[10:]
    copies = Copies(sems)

    def load(i):
        parts = xs[i][2]
        rows = ROWS // len(parts)
        return [
            copies.start(p, x_v.at[i, h * rows : (h + 1) * rows]) for h, p in enumerate(parts)
        ]

    ins = [load(0)]
    grads_in = copies.start(grads, grads_v)
    ins += [load(i) for i in range(1, 8)]
    grads_in.wait()
    done = []
    for i, (dy, sibling, _) in enumerate(xs):
        wait_all(ins[i])
        both = dot(x_v[i], grads_v[...], TN).astype(BF)
        gate_v[lanes(i)] = both[:, 0:HID]
        up_v[lanes(i)] = both[:, HID : 2 * HID]
        at = slice_at(t, dy, sibling == 1)
        done.append(copies.start(gate_v.at[lanes(i)], out_gate.at[at]))
        done.append(copies.start(up_v.at[lanes(i)], out_up.at[at]))
    wait_all(done)


def weights_down_body(t, hidden, own, sib, out, h_v, own_v, sib_v, ht_v, out_v, sems):
    copies = Copies(sems)
    h_in = copies.start(hidden, h_v)
    pairs = [(side, half) for side in range(2) for half in range(2)]
    g_in = []
    for side, half in pairs:
        cols = slice(half * 2 * COLS, (half + 1) * 2 * COLS)
        src, dst = ((own, own_v), (sib, sib_v))[side]
        g_in.append(copies.start(src.at[:, cols], dst.at[:, cols]))
    h_in.wait()
    ht_v[...] = h_v[...].T
    done = []
    for (side, half), started in zip(pairs, g_in):
        started.wait()
        cols = slice(half * 2 * COLS, (half + 1) * 2 * COLS)
        part = dot(ht_v[...], (own_v, sib_v)[side][:, cols]).astype(BF)
        for j in range(2):
            dy = half * 2 + j
            place = out_v.at[:, slice((side * 4 + dy) * COLS, (side * 4 + dy + 1) * COLS)]
            place[...] = part[:, lanes(j)]
            at = pl.ds(pl.multiple_of(slice_of(t[0], dy, side == 1) * COLS, 128), COLS)
            done.append(copies.start(place, out.at[:, at]))
    wait_all(done)


def selection(masks, at, choice=None):
    first, second, slot = masks
    hots = [one_hot(slot, e) for e in range(EXPERTS)]
    if choice is not None:
        mask = (first, second)[choice]
        hots = [hots[e] * jnp.where(mask[e : e + 1, :], 1.0, 0.0) for e in range(EXPERTS)]
    return jnp.concatenate([h[at] for h in hots], axis=0).astype(BF)


EARLY_SLOTS, LATE_SLOTS = slice(0, EARLY), slice(EARLY, CAP)


def from_slots(select, rows, cols):
    half = EXPERTS * EARLY
    return dot(select, rows[0:half, cols], TN) + dot(select, rows[half : 2 * half, cols], TN)


def combine_body(routes, rows, own, own_lanes, m1, m2, m3):
    masks = slot_masks(routes[...])
    total = from_slots(selection(masks, EARLY_SLOTS), rows, slice(0, 4 * COLS))
    own[...] = total[:, 0:COLS]
    at = slice(4 * COLS, 4 * COLS + 128)
    probs = []
    for k in range(2):
        a = from_slots(selection(masks, EARLY_SLOTS, k), rows, at)
        b = from_slots(selection(masks, LATE_SLOTS, k), rows, at)
        probs.append(a[:, 0:1] + a[:, 1:2] + b[:, 2:3] + b[:, 3:4])
    prob_lanes = split_lanes(*probs)
    own_lanes[...] = prob_lanes
    for dy, m in ((1, m1), (2, m2), (3, m3)):
        m[:, 0:COLS] = total[:, lanes(dy)].astype(BF)
        m[:, COLS : COLS + 128] = prob_lanes


def finish_body(routes, probs, rows, own, own_lanes, m1, m2, m3, out, prob_out):
    late = selection(slot_masks(routes[...]), LATE_SLOTS)
    total = from_slots(late, rows, slice(0, COLS)) + own[...]
    prob_lanes = own_lanes[...].astype(F32)
    for m in (m1, m2, m3):
        total += m[:, 0:COLS].astype(F32)
        prob_lanes += m[:, COLS : COLS + 128].astype(F32)
    out[...] = total.astype(BF)
    turned = prob_lanes.T
    p = probs[...].astype(F32)
    prob_out[0:1, :] = (turned[0:1, :] + turned[1:2, :]) / p[0:1, :]
    prob_out[1:2, :] = (turned[2:3, :] + turned[3:4, :]) / p[1:2, :]


def on_device(tokens, d_out, routes, probs, w_gate, w_up, w_down):
    wg, wu, wd = w_gate[0], w_up[0], w_down[0]
    t = lax.axis_index("tensor").astype(jnp.int32).reshape(1)
    routes_t = routes.T
    probs_t = probs.T

    def from_y(x, dy):
        return lax.ppermute(
            x, "tensor", [(i, ((i // 2 - dy) % 4) * 2 + i % 2) for i in range(8)]
        )

    def from_sibling(x):
        return lax.ppermute(x, "tensor", [(i, i ^ 1) for i in range(8)])

    def exchange(x):
        got = lax.all_to_all(x, ("dp", "ctx"), split_axis=0, concat_axis=0, tiled=True)
        return got.reshape(16 * x.shape[1], x.shape[2])

    def after(x, *others):
        return lax.optimization_barrier((x,) + others)[0]

    MB = 1 << 20
    wide = 4 * COLS
    with jax.named_scope("dispatch"):
        gs = [d_out] + [from_y(d_out, dy) for dy in (1, 2, 3)]
        send_x = call(dispatch_x_body, sds((16, CAP, COLS)), VMEM_LIMIT, flops=10**8, nbytes=MB)(routes_t, tokens)
        x0 = exchange(send_x)
        send_g = call(dispatch_g_body, sds((16, CAP, wide)), VMEM_LIMIT, flops=2 * 10**8, nbytes=4 * MB)(
            routes_t, probs_t, *gs
        )
    with jax.named_scope("gather"):
        up1, down1 = from_y(x0, 1), from_y(x0, 3)
        near_xs = [x0, up1, down1]
        near_xs += [from_sibling(x) for x in near_xs]
        far_xs = [from_y(down1[:HALF], 3), from_y(up1[HALF:], 1)]
        g_got = exchange(after(send_g, x0))
        core = t[0] % 2

        def sibling_rows(w):
            its = lax.dynamic_index_in_dim(w.reshape(4, 2, COLS, HID), 1 - core, 1, False)
            return from_sibling(after(its, x0))

        sib_wg, sib_wu = sibling_rows(wg), sibling_rows(wu)
    with jax.named_scope("forward"):
        (near,) = plain_call(
            near_forward_body,
            t,
            near_xs + [wg, wu],
            [sds((ROWS, 2 * HID), F32)],
            [((ROWS, 6 * COLS), BF), ((6 * COLS, 2 * HID), BF), ((ROWS, 2 * HID), F32)],
            40,
            1,
            1,
        )
        far_xs += [from_sibling(after(x, near)) for x in far_xs]
        g_own = after(g_got, sib_wg, sib_wu, *far_xs)
        g_sib = from_sibling(g_own)
        act, slope, hidden = plain_call(
            forward_body,
            t,
            far_xs + [near, wg, wu],
            [sds((ROWS, HID), F32), sds((ROWS, HID), F32), sds((ROWS, HID))],
            [((ROWS, 2 * COLS), BF), ((2 * COLS, 2 * HID), BF), ((ROWS, 2 * HID), F32)]
            + [((ROWS, HID), F32), ((ROWS, HID), F32), ((ROWS, HID), BF)],
            28,
            1,
            1,
        )
    with jax.named_scope("backward"):
        grads, prob = plain_call(
            back_body,
            t,
            [g_own, g_sib, act, slope, hidden, wd],
            [sds((ROWS, 2 * HID)), sds((ROWS, 128))],
            [((ROWS, wide), BF)] * 2
            + [((ROWS, HID), F32)] * 2
            + [((ROWS, HID), BF), ((HID, wide), BF), ((HID, wide), BF)]
            + [((ROWS, 2 * HID), BF), ((ROWS, 128), BF)],
            36,
            1,
            1,
        )
        grads_sib, prob_sib = from_sibling(grads), from_sibling(prob)

    def blocks(x):
        return x.reshape(16, CAP, x.shape[1])

    with jax.named_scope("sums"):
        (own_part,) = plain_call(
            own_part_body,
            t,
            [grads, wg, wu],
            [sds((ROWS, wide))],
            [((ROWS, 2 * HID), BF), ((wide, 2 * HID), BF), ((ROWS, wide), BF)],
            16,
            1,
            1,
        )
        early, *late = plain_call(
            sums_body,
            t,
            [blocks(x) for x in (own_part, grads_sib, prob, prob_sib)] + [sib_wg, sib_wu],
            [sds((16, EARLY, wide + 128))] + [sds((16, CAP - EARLY, COLS))] * 4,
            [((16, CAP, wide), BF), ((16, CAP, 2 * HID), BF)]
            + [((16, CAP, 128), BF), ((16, CAP, 128), BF)]
            + [((wide, 2 * HID), BF), ((16, EARLY, wide + 128), BF)]
            + [((4, 16, CAP - EARLY, COLS), BF)],
            44,
            1,
            1,
        )
        early_rows = exchange(early)
        arrived = [from_y(late[dy], 4 - dy) for dy in (1, 2, 3)]
    with jax.named_scope("weights_gate_up"):
        grad_gate, grad_up = plain_call(
            weights_gate_up_body,
            t,
            [after(grads, late[0])] + near_xs + far_xs,
            [sds((8 * COLS, HID))] * 2,
            [((ROWS, 2 * HID), BF), ((8, ROWS, COLS), BF)] + [((8 * COLS, HID), BF)] * 2,
            27,
            1,
            1,
        )
    with jax.named_scope("weights_down"):
        (grad_down,) = plain_call(
            weights_down_body,
            t,
            [after(hidden, grad_gate), g_own, g_sib],
            [sds((HID, 8 * COLS))],
            [((ROWS, HID), BF), ((ROWS, wide), BF), ((ROWS, wide), BF)]
            + [((HID, ROWS), BF), ((HID, 8 * COLS), BF)],
            13,
            1,
            1,
        )
    with jax.named_scope("late_sum"):
        mine = after(late[0], grad_down)
        late_sum = sum((x.astype(F32) for x in arrived), mine.astype(F32)).astype(BF)
        late_rows = exchange(late_sum)
    with jax.named_scope("finish"):
        own, own_lanes, m1, m2, m3 = call(
            combine_body,
            [sds((TOK, COLS), F32), sds((TOK, 128))] + [sds((TOK, COLS + 128))] * 3,
            SMALL_LIMIT,
            flops=1,
            nbytes=1,
        )(routes_t, early_rows)
        d_tokens, d_probs = call(
            finish_body, [sds((TOK, COLS)), sds((2, TOK), F32)], SMALL_LIMIT, flops=1, nbytes=1
        )(
            routes_t,
            probs_t,
            late_rows,
            own,
            own_lanes,
            from_y(m1, 3),
            from_y(m2, 2),
            from_y(m3, 1),
        )
    return d_tokens, d_probs.T, grad_gate[None], grad_up[None], grad_down[None]


def solution(mesh):
    in_specs = (
        P(("dp", "ctx"), "tensor"),
        P(("dp", "ctx"), "tensor"),
        P(("dp", "ctx"), None),
        P(("dp", "ctx"), None),
        P("ctx", None, ("dp", "tensor")),
        P("ctx", None, ("dp", "tensor")),
        P("ctx", ("dp", "tensor"), None),
    )
    out_specs = (
        P(("dp", "ctx"), "tensor"),
        P(("dp", "ctx"), None),
        P("ctx", None, ("dp", "tensor")),
        P("ctx", None, ("dp", "tensor")),
        P("ctx", ("dp", "tensor"), None),
    )
    return jax.shard_map(
        on_device, mesh=mesh, in_specs=in_specs, out_specs=out_specs, check_vma=False
    )
```

```python
import jax
import jax.numpy as jnp
from jax import lax
from jax.experimental import pallas as pl
from jax.experimental.pallas import tpu as pltpu
from jax.sharding import PartitionSpec as P

BF = jnp.bfloat16
F32 = jnp.float32
VMEM_LIMIT = 62 * 1024 * 1024
SMALL_LIMIT = 16 * 1024 * 1024
SHADOW_LIMIT = 56 * 1024 * 1024
EXPERTS = 8
CAP = 64
EARLY = 32
TOK = 128
COLS = 384
ROWS = 1024
HID = 512
NT = (((1,), (1,)), ((), ()))
TN = (((0,), (0,)), ((), ()))


def dot(a, b, dims=(((1,), (0,)), ((), ()))):
    return lax.dot_general(a, b, dims, preferred_element_type=F32)


def call(body, outs, limit, flops=0, nbytes=0):
    return pl.pallas_call(
        body,
        out_shape=outs,
        compiler_params=pltpu.CompilerParams(vmem_limit_bytes=limit),
        cost_estimate=pl.CostEstimate(flops=flops, bytes_accessed=nbytes, transcendentals=0),
    )


def sds(shape, dtype=BF):
    return jax.ShapeDtypeStruct(shape, dtype)


def slot_masks(routes):
    expert = lax.broadcasted_iota(jnp.int32, (EXPERTS, TOK), 0)
    first = routes[0:1, :] == expert
    second = routes[1:2, :] == expert
    named = jnp.where(first | second, 1.0, 0.0).astype(F32)
    before = lax.broadcasted_iota(jnp.int32, (TOK, TOK), 0)
    after = lax.broadcasted_iota(jnp.int32, (TOK, TOK), 1)
    earlier = jnp.where(before < after, 1.0, 0.0).astype(BF)
    rank = dot(named.astype(BF), earlier)
    slot = jnp.where(named > 0.0, rank, -1.0)
    return first, second, slot


def one_hot(slot, expert):
    place = lax.broadcasted_iota(jnp.int32, (CAP, TOK), 0).astype(F32)
    return jnp.where(slot[expert : expert + 1, :] == place, 1.0, 0.0)


def dispatch_x_body(routes, tokens, out):
    _, _, slot = slot_masks(routes[...])
    select = jnp.concatenate([one_hot(slot, e) for e in range(EXPERTS)], axis=0).astype(BF)
    rows = dot(select, tokens[...]).astype(BF).reshape(EXPERTS, CAP, COLS)
    out[0:EXPERTS] = rows
    out[EXPERTS : 2 * EXPERTS] = rows


def dispatch_g_body(routes, probs, g0, g1, g2, g3, out):
    first, _, slot = slot_masks(routes[...])
    p = probs[...].astype(F32)
    weight = jnp.where(first, p[0:1, :], p[1:2, :])
    select = jnp.concatenate(
        [one_hot(slot, e) * weight[e : e + 1, :] for e in range(EXPERTS)], axis=0
    ).astype(BF)
    for i, g in enumerate((g0, g1, g2, g3)):
        rows = dot(select, g[...]).astype(BF).reshape(EXPERTS, CAP, COLS)
        out[0:EXPERTS, :, i * COLS : (i + 1) * COLS] = rows
        out[EXPERTS : 2 * EXPERTS, :, i * COLS : (i + 1) * COLS] = rows


def slice_of(t, dy, sibling):
    core = t % 2
    core = 1 - core if sibling else core
    return ((t // 2 + dy) % 4) * 2 + core


def plain_call(body, t, ins, outs, scratch, copies, flops, nbytes, limit=VMEM_LIMIT):
    anywhere = pl.BlockSpec(memory_space=pltpu.HBM)
    return pl.pallas_call(
        body,
        out_shape=outs,
        in_specs=[pl.BlockSpec(memory_space=pltpu.SMEM)] + [anywhere] * len(ins),
        out_specs=[anywhere] * len(outs),
        scratch_shapes=[pltpu.VMEM(shape, dtype) for shape, dtype in scratch]
        + [pltpu.SemaphoreType.DMA((copies,))],
        compiler_params=pltpu.CompilerParams(vmem_limit_bytes=limit),
        cost_estimate=pl.CostEstimate(flops=flops, bytes_accessed=nbytes, transcendentals=0),
    )(t, *ins)


class Copies:
    def __init__(self, sems):
        self.sems, self.used = sems, 0

    def start(self, src, dst):
        copy = pltpu.make_async_copy(src, dst, self.sems.at[self.used])
        self.used += 1
        copy.start()
        return copy


def wait_all(copies):
    for copy in copies:
        copy.wait()


def slice_at(t, dy, sibling):
    return pl.ds(pl.multiple_of(slice_of(t[0], dy, sibling) * COLS, COLS), COLS)


def lanes(dy):
    return slice(dy * COLS, (dy + 1) * COLS)


def down_columns(copies, t, wd, into, sibling):
    return [
        copies.start(
            wd.at[:, pl.ds(pl.multiple_of(slice_of(t[0], dy, sibling) * COLS, 128), COLS)],
            into.at[:, lanes(dy)],
        )
        for dy in range(4)
    ]


def gate_up_rows(copies, t, wg, wu, into, steps, sibling):
    started = []
    for i, dy in enumerate(steps):
        at = slice_at(t, dy, sibling)
        started.append(copies.start(wg.at[at, :], into.at[lanes(i), 0:HID]))
        started.append(copies.start(wu.at[at, :], into.at[lanes(i), HID : 2 * HID]))
    return started


def chunks(rows):
    return [slice(r, r + rows) for r in range(0, ROWS, rows)]


def split_lanes(*values):
    lane = lax.broadcasted_iota(jnp.int32, values[0].shape[:-1] + (128,), values[0].ndim - 1)
    total = jnp.zeros(lane.shape, F32)
    for i, value in enumerate(values):
        upper = value.astype(BF).astype(F32)
        total = jnp.where(lane == 2 * i, upper, total)
        total = jnp.where(lane == 2 * i + 1, value - upper, total)
    return total.astype(BF)


def back_body(t, own, sib, act, slope, hidden, wd, grads, prob, *refs):
    own_v, sib_v, act_v, slope_v, hidden_v, wd_o, wd_s, grads_v, prob_v, sems = refs
    copies = Copies(sems)
    pairs = ((own, own_v), (sib, sib_v), (act, act_v), (slope, slope_v), (hidden, hidden_v))
    rows = chunks(256)
    wd_in = down_columns(copies, t, wd, wd_o, False)
    ins = [[copies.start(a.at[rows[0]], b.at[rows[0]]) for a, b in pairs]]
    wd_in += down_columns(copies, t, wd, wd_s, True)
    ins += [[copies.start(a.at[c], b.at[c]) for a, b in pairs] for c in rows[1:]]
    done = []
    for i, c in enumerate(rows):
        wait_all(ins[i])
        if i == 0:
            wait_all(wd_in[:4])
        back = dot(own_v[c], wd_o[...], NT)
        if i == 0:
            wait_all(wd_in[4:])
        back += dot(sib_v[c], wd_s[...], NT)
        prob_v[c] = split_lanes(
            jnp.sum(hidden_v[c].astype(F32) * back, axis=1, keepdims=True)
        )
        grads_v[c, 0:HID] = (back * slope_v[c]).astype(BF)
        grads_v[c, HID : 2 * HID] = (back * act_v[c]).astype(BF)
        done.append(copies.start(grads_v.at[c], grads.at[c]))
        done.append(copies.start(prob_v.at[c], prob.at[c]))
    wait_all(done)


STEP = 4


def own_part_body(t, grads, wg, wu, out, g_v, w_v, out_v, sems):
    copies = Copies(sems)
    rows = chunks(256)
    ins = [copies.start(grads.at[rows[0]], g_v.at[rows[0]])]
    w_in = gate_up_rows(copies, t, wg, wu, w_v, range(4), False)
    ins += [copies.start(grads.at[c], g_v.at[c]) for c in rows[1:]]
    wait_all(w_in)
    done = []
    for c, started in zip(rows, ins):
        started.wait()
        out_v[c] = dot(g_v[c], w_v[...], NT).astype(BF)
        done.append(copies.start(out_v.at[c], out.at[c]))
    wait_all(done)


def sums_body(t, own, grads_sib, prob, prob_sib, sib_wg, sib_wu, early, *refs):
    late, (own_v, g_v, p_v, q_v, w_v, early_v, late_v, sems) = refs[:4], refs[4:]
    copies = Copies(sems)
    blocks = [slice(i, i + STEP) for i in range(0, 16, STEP)]
    pairs = ((grads_sib, g_v), (own, own_v), (prob, p_v), (prob_sib, q_v))
    ins = [[copies.start(x.at[blocks[0]], v.at[blocks[0]]) for x, v in pairs]]
    w_in = []
    for dy in range(4):
        y = (t[0] // 2 + dy) % 4
        w_in.append(copies.start(sib_wg.at[y], w_v.at[lanes(dy), 0:HID]))
        w_in.append(copies.start(sib_wu.at[y], w_v.at[lanes(dy), HID : 2 * HID]))
    ins += [[copies.start(x.at[b], v.at[b]) for x, v in pairs] for b in blocks[1:]]
    wait_all(w_in)
    done = []
    for b, started in zip(blocks, ins):
        wait_all(started)
        part = dot(g_v[b].reshape(STEP * CAP, 2 * HID), w_v[...], NT)
        for dy in range(4):
            value = part[:, lanes(dy)].reshape(STEP, CAP, COLS)
            value = (value + own_v[b, :, lanes(dy)].astype(F32)).astype(BF)
            early_v[b, :, lanes(dy)] = value[:, 0:EARLY]
            late_v[dy, b] = value[:, EARLY:CAP]
        both = p_v[b].astype(F32) + q_v[b].astype(F32)
        both = jnp.sum(both, axis=2, keepdims=True)
        early_v[b, :, 4 * COLS : 4 * COLS + 128] = split_lanes(
            both[:, 0:EARLY], both[:, EARLY:CAP]
        )
        done.append(copies.start(early_v.at[b], early.at[b]))
        for dy in range(4):
            done.append(copies.start(late_v.at[dy, b], late[dy].at[b]))
    wait_all(done)


HALF = ROWS // 2


def part_of(source, c):
    if len(source) == 1:
        return source[0].at[c]
    half = c.start // HALF
    return source[half].at[slice(c.start - half * HALF, c.stop - half * HALF)]


def in_chunks(copies, sources, x_v, c):
    return [copies.start(part_of(x, c), x_v.at[c, lanes(i)]) for i, x in enumerate(sources)]


def near_forward_body(t, *refs):
    xs, wg, wu, out = [(x,) for x in refs[:6]], refs[6], refs[7], refs[8]
    x_v, w_v, out_v, sems = refs[9:]
    copies = Copies(sems)
    w_in = gate_up_rows(copies, t, wg, wu, w_v.at[0 : 3 * COLS], (0, 1, 3), False)
    w_in += gate_up_rows(copies, t, wg, wu, w_v.at[3 * COLS : 6 * COLS], (0, 1, 3), True)
    rows = chunks(256)
    ins = [in_chunks(copies, xs, x_v, c) for c in rows]
    wait_all(w_in)
    done = []
    for i, c in enumerate(rows):
        wait_all(ins[i])
        out_v[c] = dot(x_v[c], w_v[...])
        done.append(copies.start(out_v.at[c], out.at[c]))
    wait_all(done)


def forward_body(t, *refs):
    xs, near, wg, wu = [refs[0:2], refs[2:4]], *refs[4:7]
    act, slope, hidden, x_v, w_v, near_v, act_v, slope_v, hidden_v, sems = refs[7:]
    copies = Copies(sems)
    w_in = gate_up_rows(copies, t, wg, wu, w_v.at[0:COLS], (2,), False)
    w_in += gate_up_rows(copies, t, wg, wu, w_v.at[COLS : 2 * COLS], (2,), True)
    rows = chunks(256)
    ins = [
        in_chunks(copies, xs, x_v, c) + [copies.start(near.at[c], near_v.at[c])] for c in rows
    ]
    wait_all(w_in)
    done = []
    for i, c in enumerate(rows):
        wait_all(ins[i])
        total = near_v[c] + dot(x_v[c], w_v[...])
        gate, up = total[:, 0:HID], total[:, HID : 2 * HID]
        sigma = jax.nn.sigmoid(gate)
        active = gate * sigma
        act_v[c] = active
        slope_v[c] = up * (sigma * (1.0 + gate * (1.0 - sigma)))
        hidden_v[c] = (active * up).astype(BF)
        for a, b in ((act_v, act), (slope_v, slope), (hidden_v, hidden)):
            done.append(copies.start(a.at[c], b.at[c]))
    wait_all(done)


def weights_gate_up_body(t, grads, *refs):
    xs = [(0, 0, refs[0:1]), (1, 0, refs[1:2]), (3, 0, refs[2:3])]
    xs += [(0, 1, refs[3:4]), (1, 1, refs[4:5]), (3, 1, refs[5:6])]
    xs += [(2, 0, refs[6:8]), (2, 1, refs[8:10])]
    out_gate, out_up, grads_v, x_v, gate_v, up_v, sems = refs[10:]
    copies = Copies(sems)

    def load(i):
        parts = xs[i][2]
        rows = ROWS // len(parts)
        return [
            copies.start(p, x_v.at[i, h * rows : (h + 1) * rows]) for h, p in enumerate(parts)
        ]

    ins = [load(0)]
    grads_in = copies.start(grads, grads_v)
    ins += [load(i) for i in range(1, 8)]
    grads_in.wait()
    done = []
    for i, (dy, sibling, _) in enumerate(xs):
        wait_all(ins[i])
        both = dot(x_v[i], grads_v[...], TN).astype(BF)
        gate_v[lanes(i)] = both[:, 0:HID]
        up_v[lanes(i)] = both[:, HID : 2 * HID]
        at = slice_at(t, dy, sibling == 1)
        done.append(copies.start(gate_v.at[lanes(i)], out_gate.at[at]))
        done.append(copies.start(up_v.at[lanes(i)], out_up.at[at]))
    wait_all(done)


def weights_down_body(t, hidden, own, sib, out, h_v, own_v, sib_v, ht_v, out_v, sems):
    copies = Copies(sems)
    h_in = copies.start(hidden, h_v)
    pairs = [(side, half) for side in range(2) for half in range(2)]
    g_in = []
    for side, half in pairs:
        cols = slice(half * 2 * COLS, (half + 1) * 2 * COLS)
        src, dst = ((own, own_v), (sib, sib_v))[side]
        g_in.append(copies.start(src.at[:, cols], dst.at[:, cols]))
    h_in.wait()
    ht_v[...] = h_v[...].T
    done = []
    for (side, half), started in zip(pairs, g_in):
        started.wait()
        cols = slice(half * 2 * COLS, (half + 1) * 2 * COLS)
        part = dot(ht_v[...], (own_v, sib_v)[side][:, cols]).astype(BF)
        for j in range(2):
            dy = half * 2 + j
            place = out_v.at[:, slice((side * 4 + dy) * COLS, (side * 4 + dy + 1) * COLS)]
            place[...] = part[:, lanes(j)]
            at = pl.ds(pl.multiple_of(slice_of(t[0], dy, side == 1) * COLS, 128), COLS)
            done.append(copies.start(place, out.at[:, at]))
    wait_all(done)


def selection(masks, at, choice=None):
    first, second, slot = masks
    hots = [one_hot(slot, e) for e in range(EXPERTS)]
    if choice is not None:
        mask = (first, second)[choice]
        hots = [hots[e] * jnp.where(mask[e : e + 1, :], 1.0, 0.0) for e in range(EXPERTS)]
    return jnp.concatenate([h[at] for h in hots], axis=0).astype(BF)


EARLY_SLOTS, LATE_SLOTS = slice(0, EARLY), slice(EARLY, CAP)


def from_slots(select, rows, cols):
    half = EXPERTS * EARLY
    return dot(select, rows[0:half, cols], TN) + dot(select, rows[half : 2 * half, cols], TN)


def combine_body(routes, rows, own, own_lanes, m1, m2, m3):
    masks = slot_masks(routes[...])
    total = from_slots(selection(masks, EARLY_SLOTS), rows, slice(0, 4 * COLS))
    own[...] = total[:, 0:COLS]
    at = slice(4 * COLS, 4 * COLS + 128)
    probs = []
    for k in range(2):
        a = from_slots(selection(masks, EARLY_SLOTS, k), rows, at)
        b = from_slots(selection(masks, LATE_SLOTS, k), rows, at)
        probs.append(a[:, 0:1] + a[:, 1:2] + b[:, 2:3] + b[:, 3:4])
    prob_lanes = split_lanes(*probs)
    own_lanes[...] = prob_lanes
    for dy, m in ((1, m1), (2, m2), (3, m3)):
        m[:, 0:COLS] = total[:, lanes(dy)].astype(BF)
        m[:, COLS : COLS + 128] = prob_lanes


def finish_body(routes, probs, rows, own, own_lanes, m1, m2, m3, out, prob_out):
    late = selection(slot_masks(routes[...]), LATE_SLOTS)
    total = from_slots(late, rows, slice(0, COLS)) + own[...]
    prob_lanes = own_lanes[...].astype(F32)
    for m in (m1, m2, m3):
        total += m[:, 0:COLS].astype(F32)
        prob_lanes += m[:, COLS : COLS + 128].astype(F32)
    out[...] = total.astype(BF)
    turned = prob_lanes.T
    p = probs[...].astype(F32)
    prob_out[0:1, :] = (turned[0:1, :] + turned[1:2, :]) / p[0:1, :]
    prob_out[1:2, :] = (turned[2:3, :] + turned[3:4, :]) / p[1:2, :]


def on_device(tokens, d_out, routes, probs, w_gate, w_up, w_down):
    wg, wu, wd = w_gate[0], w_up[0], w_down[0]
    t = lax.axis_index("tensor").astype(jnp.int32).reshape(1)
    routes_t = routes.T
    probs_t = probs.T

    def from_y(x, dy):
        return lax.ppermute(
            x, "tensor", [(i, ((i // 2 - dy) % 4) * 2 + i % 2) for i in range(8)]
        )

    def from_sibling(x):
        return lax.ppermute(x, "tensor", [(i, i ^ 1) for i in range(8)])

    def exchange(x):
        got = lax.all_to_all(x, ("dp", "ctx"), split_axis=0, concat_axis=0, tiled=True)
        return got.reshape(16 * x.shape[1], x.shape[2])

    def after(x, *others):
        return lax.optimization_barrier((x,) + others)[0]

    MB = 1 << 20
    wide = 4 * COLS
    with jax.named_scope("dispatch"):
        gs = [d_out] + [from_y(d_out, dy) for dy in (1, 2, 3)]
        send_x = call(dispatch_x_body, sds((16, CAP, COLS)), VMEM_LIMIT, flops=10**8, nbytes=MB)(routes_t, tokens)
        x0 = exchange(send_x)
        send_g = call(dispatch_g_body, sds((16, CAP, wide)), VMEM_LIMIT, flops=2 * 10**8, nbytes=4 * MB)(
            routes_t, probs_t, *gs
        )
    with jax.named_scope("gather"):
        up1, down1 = from_y(x0, 1), from_y(x0, 3)
        near_xs = [x0, up1, down1]
        near_xs += [from_sibling(x) for x in near_xs]
        far_xs = [from_y(down1[:HALF], 3), from_y(up1[HALF:], 1)]
        g_got = exchange(after(send_g, x0))
        core = t[0] % 2

        def sibling_rows(w):
            its = lax.dynamic_index_in_dim(w.reshape(4, 2, COLS, HID), 1 - core, 1, False)
            return from_sibling(after(its, x0))

        sib_wg, sib_wu = sibling_rows(wg), sibling_rows(wu)
    with jax.named_scope("forward"):
        (near,) = plain_call(
            near_forward_body,
            t,
            near_xs + [wg, wu],
            [sds((ROWS, 2 * HID), F32)],
            [((ROWS, 6 * COLS), BF), ((6 * COLS, 2 * HID), BF), ((ROWS, 2 * HID), F32)],
            40,
            1,
            1,
        )
        far_xs += [from_sibling(after(x, near)) for x in far_xs]
        g_own = after(g_got, sib_wg, sib_wu, *far_xs)
        g_sib = from_sibling(g_own)
        act, slope, hidden = plain_call(
            forward_body,
            t,
            far_xs + [near, wg, wu],
            [sds((ROWS, HID), F32), sds((ROWS, HID), F32), sds((ROWS, HID))],
            [((ROWS, 2 * COLS), BF), ((2 * COLS, 2 * HID), BF), ((ROWS, 2 * HID), F32)]
            + [((ROWS, HID), F32), ((ROWS, HID), F32), ((ROWS, HID), BF)],
            28,
            1,
            1,
        )
    with jax.named_scope("backward"):
        grads, prob = plain_call(
            back_body,
            t,
            [g_own, g_sib, act, slope, hidden, wd],
            [sds((ROWS, 2 * HID)), sds((ROWS, 128))],
            [((ROWS, wide), BF)] * 2
            + [((ROWS, HID), F32)] * 2
            + [((ROWS, HID), BF), ((HID, wide), BF), ((HID, wide), BF)]
            + [((ROWS, 2 * HID), BF), ((ROWS, 128), BF)],
            36,
            1,
            1,
        )
        grads_sib, prob_sib = from_sibling(grads), from_sibling(prob)

    def blocks(x):
        return x.reshape(16, CAP, x.shape[1])

    with jax.named_scope("sums"):
        (own_part,) = plain_call(
            own_part_body,
            t,
            [grads, wg, wu],
            [sds((ROWS, wide))],
            [((ROWS, 2 * HID), BF), ((wide, 2 * HID), BF), ((ROWS, wide), BF)],
            16,
            1,
            1,
        )
        early, *late = plain_call(
            sums_body,
            t,
            [blocks(x) for x in (own_part, grads_sib, prob, prob_sib)] + [sib_wg, sib_wu],
            [sds((16, EARLY, wide + 128))] + [sds((16, CAP - EARLY, COLS))] * 4,
            [((16, CAP, wide), BF), ((16, CAP, 2 * HID), BF)]
            + [((16, CAP, 128), BF), ((16, CAP, 128), BF)]
            + [((wide, 2 * HID), BF), ((16, EARLY, wide + 128), BF)]
            + [((4, 16, CAP - EARLY, COLS), BF)],
            44,
            1,
            1,
        )
        early_rows = exchange(early)
        arrived = [from_y(late[dy], 4 - dy) for dy in (1, 2, 3)]
    with jax.named_scope("weights_gate_up"):
        grad_gate, grad_up = plain_call(
            weights_gate_up_body,
            t,
            [after(grads, late[0])] + near_xs + far_xs,
            [sds((8 * COLS, HID))] * 2,
            [((ROWS, 2 * HID), BF), ((8, ROWS, COLS), BF)] + [((8 * COLS, HID), BF)] * 2,
            27,
            1,
            1,
            SHADOW_LIMIT,
        )
    with jax.named_scope("weights_down"):
        (grad_down,) = plain_call(
            weights_down_body,
            t,
            [after(hidden, grad_gate), g_own, g_sib],
            [sds((HID, 8 * COLS))],
            [((ROWS, HID), BF), ((ROWS, wide), BF), ((ROWS, wide), BF)]
            + [((HID, ROWS), BF), ((HID, 8 * COLS), BF)],
            13,
            1,
            1,
            SHADOW_LIMIT,
        )
    with jax.named_scope("late_sum"):
        mine = after(late[0], grad_down)
        late_sum = sum((x.astype(F32) for x in arrived), mine.astype(F32)).astype(BF)
        late_rows = exchange(late_sum)
    with jax.named_scope("finish"):
        own, own_lanes, m1, m2, m3 = call(
            combine_body,
            [sds((TOK, COLS), F32), sds((TOK, 128))] + [sds((TOK, COLS + 128))] * 3,
            SMALL_LIMIT,
            flops=1,
            nbytes=1,
        )(routes_t, early_rows)
        d_tokens, d_probs = call(
            finish_body, [sds((TOK, COLS)), sds((2, TOK), F32)], SMALL_LIMIT, flops=1, nbytes=1
        )(
            routes_t,
            probs_t,
            late_rows,
            own,
            own_lanes,
            from_y(m1, 3),
            from_y(m2, 2),
            from_y(m3, 1),
        )
    return d_tokens, d_probs.T, grad_gate[None], grad_up[None], grad_down[None]


def solution(mesh):
    in_specs = (
        P(("dp", "ctx"), "tensor"),
        P(("dp", "ctx"), "tensor"),
        P(("dp", "ctx"), None),
        P(("dp", "ctx"), None),
        P("ctx", None, ("dp", "tensor")),
        P("ctx", None, ("dp", "tensor")),
        P("ctx", ("dp", "tensor"), None),
    )
    out_specs = (
        P(("dp", "ctx"), "tensor"),
        P(("dp", "ctx"), None),
        P("ctx", None, ("dp", "tensor")),
        P("ctx", None, ("dp", "tensor")),
        P("ctx", ("dp", "tensor"), None),
    )
    return jax.shard_map(
        on_device, mesh=mesh, in_specs=in_specs, out_specs=out_specs, check_vma=False
    )
```
